256 devices in a mesh: tensor: 32 (over x, z), dp: 8 (over y, core).
Axes of the slice: x: 4, y: 4, z: 8, core: 2. Of those that a mesh axis runs over, the one named last changes fastest.
Arguments:
- hidden: bfloat16 [8192, 15360], P('dp', 'tensor'), parts along dimension 0, may hold values from -6 to 6
- residual: bfloat16 [8192, 8192], P(('dp', 'tensor')), parts along dimension 0, may hold values from -24 to 24
- down_weight: bfloat16 [15360, 8192], P('tensor'), may hold values from -0.046875 to 0.046875
- norm_gain: bfloat16 [8192], replicated, may hold values from 0.099609375 to 1.8984375
- query_codes: bfloat16 [8192, 4096], P(None, 'tensor'), may hold values from -4 to 4
- query_scales: bfloat16 [64, 4096], P(None, 'tensor'), may hold values from 0.0010986328 to 0.0043945312
- pair_codes: bfloat16 [2, 8192, 1024], P(None, None, 'tensor'), may hold values from -4 to 4
- pair_scales: bfloat16 [2, 64, 1024], P(None, None, 'tensor'), may hold values from 0.0010986328 to 0.0043945312
- input_groups: int32 [8192], replicated, may hold values from 0 to 63, as said below
- query_bias: bfloat16 [4096], P('tensor'), may hold values from -3 to 3
- pair_bias: bfloat16 [2, 1024], P(None, 'tensor'), may hold values from -3 to 3
Outputs:
- new_residual: bfloat16 [8192, 8192], P(('dp', 'tensor')), parts along dimension 0
- queries: bfloat16 [8192, 4096], P('dp', 'tensor'), parts along dimension 0
- key_values: bfloat16 [2, 8192, 1024], P(None, 'dp', 'tensor'), parts along dimension 1
The draws below stay inside these ranges and needn't reach their ends.
There are 8 independent parts, one for each index of `dp`. The reference program is written for one: setup_inputs(seed, part) draws one part's arguments, and reference() takes and returns one part's arrays. A program takes and returns all parts, laid end to end along the dimension named above; an argument that names none is the same for every part. Nothing has to cross between parts.
Inputs may be any that keep to these rules, and one draw needn't show every extreme that they name: `input_groups`: each value is the quantization group of one model feature; every group of 0 to 63 holds exactly 128 features.
All inputs are finite; a program needn't handle non-finite values.
Results may differ from the reference program's by a relative error of at most 0.02.
Values may be sent and summed in bfloat16 or wider, within the bound.
A program may use at most 192 MiB of HBM per device.

```python
import math
import jax
import jax.numpy as jnp
from jax import lax

D = 8192
FF = 15360
GROUP = 128
TOK_DEV = 32
TOKENS = 1024
QCOLS = 4096
KV = 1024
N_TENSOR = 32


def draw_residual(key, part):
    key = jax.random.fold_in(key, 11)
    column_key, row_key, value_key = jax.random.split(key, 3)
    columns = jnp.exp(jax.random.uniform(column_key, (D,), jnp.float32, math.log(0.3), math.log(3.0)))
    row_scale = jnp.exp(jax.random.uniform(row_key, (TOKENS, 1), jnp.float32, math.log(0.5), math.log(2.0)))
    values = jnp.clip(jax.random.normal(value_key, (TOKENS, D), jnp.float32), -4.0, 4.0)
    return (values * row_scale * columns[None, :]).astype(jnp.bfloat16)


def draw_input_groups(key, part):
    key = jax.random.fold_in(key, 7)
    return (jax.random.permutation(key, D) // GROUP).astype(jnp.int32)


def strengthened(result, stream_key, source, target, shards_of, factor):
    def block_of(axis_at):
        return (jnp.arange(result.shape[axis_at]) // (result.shape[axis_at] // shards_of)).reshape((-1,) + (1,) * (result.ndim - 1 - axis_at))

    one_side = jax.random.permutation(stream_key, shards_of)[block_of(target)]
    second = (block_of(target) + shards_of // 2) % shards_of
    return jnp.where((block_of(source) == one_side) | (block_of(source) == second), factor * result, result)


def levels(rng, shape, pieces, low, top_value):
    level, own = 1.0, jax.random.fold_in(rng, 6)
    for dim, shards_of in pieces:
        draws = jnp.exp(jax.random.uniform(jax.random.fold_in(own, dim), (shards_of,), jnp.float32, low / len(pieces), top_value / len(pieces)))
        level = level * jnp.repeat(draws, shape[dim] // shards_of).reshape([-1 if axis == dim else 1 for axis in range(len(shape))])
    return level


def noise(own_key, dims, deviation, limit, pieces=(), kind=jnp.bfloat16):
    level = levels(own_key, dims, pieces, -0.22, 0.18) if pieces else 1.0
    drawn = jax.random.normal(own_key, dims, jnp.float32) * deviation * level
    return jnp.minimum(jnp.maximum(drawn, -limit), limit).astype(kind)


def gaussian_with(rng, extent, scale, bound, shards, heavy, held_as=jnp.bfloat16):
    drawn = scale * jax.random.normal(rng, extent, jnp.float32)
    if shards:
        drawn = drawn * levels(rng, extent, shards, -0.22, 0.18)
    return jnp.clip(strengthened(drawn, jax.random.fold_in(rng, 3), *heavy), -bound, bound).astype(held_as)


def setup_inputs(seed: int = 0, part: int = 0) -> dict:
    streams_of = jax.random.split(jax.random.key(seed), 12)
    part_keys = jax.random.split(jax.random.fold_in(streams_of[11], part), 12)
    return {
        "hidden": gaussian_with(part_keys[0], (TOKENS, FF), 1.0, 6.0, ((1, 32),), (1, 0, 32, 2.75)),
        "residual": draw_residual(jax.random.fold_in(jax.random.fold_in(streams_of[11], part), 71), part),
        "down_weight": noise(streams_of[2], (FF, D), FF ** -0.5, 0.046875, ((0, 32),)),
        "norm_gain": jnp.clip(1.0 + 0.18 * jax.random.normal(streams_of[3], (D,), jnp.float32), 0.099609375, 1.8984375).astype(jnp.bfloat16),
        "query_codes": noise(streams_of[4], (D, QCOLS), 1.0, 4.0, ((1, 32),)),
        "query_scales": jnp.clip(jnp.exp(math.log(0.0043945312) - 1.3862944 * jax.random.uniform(streams_of[5], (D // GROUP, QCOLS), jnp.float32) ** levels(streams_of[5], (D // GROUP, QCOLS), ((1, 32),), -0.2, 0.2)), 0.0010986328, 0.0043945312).astype(jnp.bfloat16),
        "pair_codes": noise(streams_of[6], (2, D, KV), 1.0, 4.0, ((2, 32),)),
        "pair_scales": jnp.clip(jnp.exp(math.log(0.0043945312) - 1.3862944 * jax.random.uniform(streams_of[7], (2, D // GROUP, KV), jnp.float32) ** levels(streams_of[7], (2, D // GROUP, KV), ((2, 32),), -0.2, 0.2)), 0.0010986328, 0.0043945312).astype(jnp.bfloat16),
        "input_groups": draw_input_groups(jax.random.fold_in(streams_of[11], 71), part),
        "query_bias": noise(streams_of[9], (QCOLS,), 0.5, 3.0, ((0, 32),)),
        "pair_bias": noise(streams_of[10], (2, KV), 0.5, 3.0, ((1, 32),)),
    }


def dequant(codes, scale_rows):
    return (codes.astype(jnp.float32) * scale_rows.astype(jnp.float32)).astype(jnp.bfloat16)

def reference(hidden, residual, down_weight, norm_gain, query_codes, query_scales, pair_codes, pair_scales, input_groups, query_bias, pair_bias):
    shard_rows = FF // N_TENSOR

    def add_shard(running, owner):
        first = owner * shard_rows
        weight = lax.dynamic_slice_in_dim(down_weight, first, shard_rows, 0)
        inputs = lax.dynamic_slice_in_dim(hidden, first, shard_rows, 1)
        partial_value = jnp.dot(inputs, weight, preferred_element_type=jnp.float32)
        token_first = owner * TOK_DEV
        own_rows = lax.dynamic_slice_in_dim(partial_value, token_first, TOK_DEV, 0)
        own_rows = own_rows + lax.dynamic_slice_in_dim(residual, token_first, TOK_DEV, 0).astype(jnp.float32)
        partial_value = lax.dynamic_update_slice_in_dim(partial_value, own_rows, token_first, 0)
        rounded = lax.optimization_barrier(partial_value.astype(jnp.bfloat16))
        return (running + rounded.astype(jnp.float32), None)
    summed, _ = lax.scan(add_shard, jnp.zeros((TOKENS, D), jnp.float32), jnp.arange(N_TENSOR, dtype=jnp.int32))
    new_residual = summed.astype(jnp.bfloat16)
    widened = new_residual.astype(jnp.float32)
    normed = (widened * lax.rsqrt(lax.optimization_barrier(jnp.mean(widened * widened, axis=1, keepdims=True)) + 1e-06) * norm_gain.astype(jnp.float32)).astype(jnp.bfloat16)
    query_weight = dequant(query_codes, jnp.take(query_scales, input_groups, axis=0))
    queries = (jnp.dot(normed, query_weight, preferred_element_type=jnp.float32) + query_bias.astype(jnp.float32)).astype(jnp.bfloat16)
    outputs = []
    for which in range(2):
        weight = dequant(pair_codes[which], jnp.take(pair_scales[which], input_groups, axis=0))
        outputs.append((jnp.dot(normed, weight, preferred_element_type=jnp.float32) + pair_bias[which].astype(jnp.float32)).astype(jnp.bfloat16))
    return (new_residual, queries, jnp.stack(outputs))
```

```python
import functools

import jax
import jax.numpy as jnp
from jax import lax
from jax.experimental import pallas as pl
from jax.experimental.pallas import tpu as pltpu
from jax.sharding import PartitionSpec as P

MESH = pl.DeviceIdType.MESH
NX, NZ, NY, NC = 4, 8, 4, 2
F32, BF16 = jnp.float32, jnp.bfloat16
HALF = 1024
SUB = 512
AHEAD = 3


def kernel(
    hid, res, w, wq, bias, nr_out, q_out, kv_out,
    wb, hb, rsb, yb, wqb, part, snd, resb,
    l_h, l_w, l_r, l_q, l_n,
    h_s, h_r, w_s, w_r, wy_s, wy_r, wc_s, wc_r, q_s, q_r, qy_s, qy_r, qc_s, qc_r,
    r_s, r_r, rs_s, rs_r, ag_s, ag_r, n_s, n_r, p_s, p_r,
):
    t, d = lax.axis_index("tensor"), lax.axis_index("dp")
    x, z = t // NZ, t % NZ
    y, c = d // NC, d % NC

    def at(xx, zz, yy, cc):
        return {"tensor": xx * NZ + zz, "dp": yy * NC + cc}

    def to_x(o):
        return at((x + o) % NX, z, y, c)

    def to_z(o):
        return at(x, (z + o + NZ) % NZ, y, c)

    def to_y(o):
        return at(x, z, (y + o) % NY, c)

    sibling = at(x, z, y, 1 - c)

    def remote(src, dst, ss, rs, device):
        return pltpu.make_async_remote_copy(
            src_ref=src, dst_ref=dst, send_sem=ss, recv_sem=rs, device_id=device, device_id_type=MESH
        )

    def xs(o):
        return (x + o) % NX

    rank = c * NY + y
    def hid_local(u):
        zl, zh = (z + 2 * NZ - 1 - u) % NZ, (z + 1 + u) % NZ
        return (
            pltpu.make_async_copy(hid.at[pl.ds(0, 2), zl], hb.at[x, u, pl.ds(0, 2)], l_h.at[u, 0]),
            pltpu.make_async_copy(hid.at[pl.ds(2, 2), zh], hb.at[x, u, pl.ds(2, 2)], l_h.at[u, 1]),
        )

    def w_local(r):
        return pltpu.make_async_copy(w.at[:, pl.ds(x * 2 * HALF + r * HALF, HALF)], wb.at[r, x], l_w.at[r])

    def res_local():
        return pltpu.make_async_copy(res.at[:, pl.ds(x * 2 * HALF, 2 * HALF)], resb.at[x], l_r.at[0])

    def wq_local():
        return pltpu.make_async_copy(
            wq.at[x], wqb.at[:, pl.ds(rank * 128, 128), pl.ds(x * 256, 256)], l_q.at[0]
        )

    def nr_local(r):
        return pltpu.make_async_copy(
            yb.at[r, 0, x], nr_out.at[:, pl.ds(x * 2 * HALF + r * HALF, HALF)], l_n.at[r]
        )

    def h_direct(u, side):
        o = 1 if side == 0 else 3
        return remote(hb.at[x, u], hb.at[x, u], h_s.at[u, side], h_r.at[u, side], to_x(o))

    def h_direct_in(u, side):
        o = 3 if side == 0 else 1
        ref = hb.at[xs(o), u]
        return remote(ref, ref, h_s.at[u, side], h_r.at[u, side], to_x(o))

    def h_forward(u, side):
        src = xs(3) if side == 0 else xs(1)
        ref = hb.at[src, u, pl.ds(2 * side, 2)]
        return remote(ref, ref, h_s.at[u, 2 + side], h_r.at[u, 2 + side], to_x(1 if side == 0 else 3))

    def h_forward_in(u, side):
        ref = hb.at[xs(2), u, pl.ds(2 * side, 2)]
        return remote(ref, ref, h_s.at[u, 2 + side], h_r.at[u, 2 + side], to_x(2))

    def w_x(r, o):
        cols = pl.ds(xs(o) * 2 * HALF + r * HALF + rank * 128, 128)
        return remote(
            w.at[:, cols], wb.at[r, x, :, pl.ds(rank * 128, 128)], w_s.at[r, o - 1], w_r.at[r, o - 1], to_x(o)
        )

    def w_x_in(r, o):
        ref = wb.at[r, xs(NX - o), :, pl.ds(rank * 128, 128)]
        return remote(ref, ref, w_s.at[r, o - 1], w_r.at[r, o - 1], to_x(o))

    def w_y(r, o, p):
        ref = wb.at[r, xs(NX - o), :, pl.ds(rank * 128, 128)]
        return remote(ref, ref, wy_s.at[r, o - 1, p - 1], wy_r.at[r, o - 1, p - 1], to_y(p))

    def w_y_in(r, o, p):
        other = c * NY + (y + NY - p) % NY
        ref = wb.at[r, xs(NX - o), :, pl.ds(other * 128, 128)]
        return remote(ref, ref, wy_s.at[r, o - 1, p - 1], wy_r.at[r, o - 1, p - 1], to_y(p))

    def w_c(r, o):
        ref = wb.at[r, xs(NX - o), :, pl.ds(c * 512, 512)]
        return remote(ref, ref, wc_s.at[r, o - 1], wc_r.at[r, o - 1], sibling)

    def w_c_in(r, o):
        ref = wb.at[r, xs(NX - o), :, pl.ds((1 - c) * 512, 512)]
        return remote(ref, ref, wc_s.at[r, o - 1], wc_r.at[r, o - 1], sibling)

    def q_x(o):
        dst = wqb.at[:, pl.ds(rank * 128, 128), pl.ds(x * 256, 256)]
        return remote(wq.at[xs(o)], dst, q_s.at[o - 1], q_r.at[o - 1], to_x(o))

    def q_x_in(o):
        ref = wqb.at[:, pl.ds(rank * 128, 128), pl.ds(xs(NX - o) * 256, 256)]
        return remote(ref, ref, q_s.at[o - 1], q_r.at[o - 1], to_x(o))

    def q_y(p):
        ref = wqb.at[:, pl.ds(rank * 128, 128), :]
        return remote(ref, ref, qy_s.at[p - 1], qy_r.at[p - 1], to_y(p))

    def q_y_in(p):
        other = c * NY + (y + NY - p) % NY
        ref = wqb.at[:, pl.ds(other * 128, 128), :]
        return remote(ref, ref, qy_s.at[p - 1], qy_r.at[p - 1], to_y(p))

    def q_c():
        ref = wqb.at[:, pl.ds(c * 512, 512), :]
        return remote(ref, ref, qc_s.at[0], qc_r.at[0], sibling)

    def q_c_in():
        ref = wqb.at[:, pl.ds((1 - c) * 512, 512), :]
        return remote(ref, ref, qc_s.at[0], qc_r.at[0], sibling)

    def res_x(o):
        return remote(
            res.at[:, pl.ds(xs(o) * 2 * HALF, 2 * HALF)], resb.at[x], r_s.at[o - 1], r_r.at[o - 1], to_x(o)
        )

    def res_x_in(o):
        ref = resb.at[xs(NX - o)]
        return remote(ref, ref, r_s.at[o - 1], r_r.at[o - 1], to_x(o))

    def ring(buf, ss, rs, r, k, side, j):
        rows, cols = pl.ds(2 * side, 2), pl.ds(j * SUB, SUB)
        return remote(
            buf.at[r, k, rows, :, cols], buf.at[r, k + 1, rows, :, cols],
            ss.at[r, k, side, j], rs.at[r, k, side, j], to_z(1 if side == 0 else -1),
        )

    def ring_in(buf, ss, rs, r, k, side, j):
        rows, cols = pl.ds(2 * side, 2), pl.ds(j * SUB, SUB)
        ref = buf.at[r, k, rows, :, cols]
        return remote(ref, ref, ss.at[r, k - 1, side, j], rs.at[r, k - 1, side, j], to_z(1))

    def nr_x(r, o):
        return remote(
            yb.at[r, 0, xs(o)], nr_out.at[:, pl.ds(x * 2 * HALF + r * HALF, HALF)],
            n_s.at[r, o - 1], n_r.at[r, o - 1], to_x(o),
        )

    def nr_x_in(r, o):
        ref = nr_out.at[:, pl.ds(xs(NX - o) * 2 * HALF + r * HALF, HALF)]
        return remote(ref, ref, n_s.at[r, o - 1], n_r.at[r, o - 1], to_x(o))

    def part_x(k, o):
        return remote(snd.at[k, xs(o)], part.at[o - 1, k], p_s.at[k, o - 1], p_r.at[k, o - 1], to_x(o))

    def own_send(u):
        for copy in hid_local(u):
            copy.wait()
        for side in range(2):
            h_direct(u, side).start()

    def front(u):
        for side in range(2):
            h_direct_in(u, side).wait_recv()
            h_forward(u, side).start()

    def back(u):
        for side in range(2):
            h_forward_in(u, side).wait_recv()

    def w_spread_y(r):
        for o in (1, 3, 2):
            w_x_in(r, o).wait_recv()
            for p in (1, 3, 2):
                w_y(r, o, p).start()

    def w_spread_c(r):
        for o in (1, 3, 2):
            for p in (1, 3, 2):
                w_y_in(r, o, p).wait_recv()
            w_c(r, o).start()

    def w_ready(r):
        w_local(r).wait()
        for o in (1, 3, 2):
            w_c_in(r, o).wait_recv()

    def reduce_step(r, k):
        for j in range(2):
            cols = pl.ds(j * SUB, SUB)
            acc = jnp.zeros((128, SUB), F32)
            for xx in range(NX):
                acc += jnp.dot(
                    hb[xx, k].reshape(128, hb.shape[-1]), wb[r, xx, :, cols], preferred_element_type=F32
                )

            @pl.when(k > 0)
            def _():
                for side in range(2):
                    ring_in(rsb, rs_s, rs_r, r, k, side, j).wait_recv()

            acc += rsb[r, k, :, :, cols].reshape(128, SUB).astype(F32)

            @pl.when(k < NZ - 1)
            def _():
                rsb[r, k, :, :, cols] = acc.astype(BF16).reshape(4, 32, SUB)
                for side in range(2):
                    ring(rsb, rs_s, rs_r, r, k, side, j).start()

            @pl.when(k == NZ - 1)
            def _():
                own = resb[:, :, pl.ds(r * HALF + j * SUB, SUB)].reshape(128, SUB).astype(F32)
                yb[r, 0, :, :, cols] = (acc + own).astype(BF16).reshape(4, 32, SUB)

    def gather_step(r, k):
        for j in range(2):
            @pl.when(k > 0)
            def _():
                for side in range(2):
                    ring_in(yb, ag_s, ag_r, r, k, side, j).wait_recv()

            @pl.when(k < NZ - 1)
            def _():
                for side in range(2):
                    ring(yb, ag_s, ag_r, r, k, side, j).start()

    def residual_out(r):
        nr_local(r).start()
        for o in (1, 3, 2):
            nr_x(r, o).start()

    def project_step(k):
        acc = jnp.zeros((128, NX * 256), F32)
        squares = jnp.zeros((128, 1), F32)
        for r in range(2):
            rows = yb[r, k].reshape(128, HALF)
            acc += jnp.dot(rows, wqb[r], preferred_element_type=F32)
            wide = rows.astype(F32)
            squares += jnp.sum(wide * wide, axis=1, keepdims=True)
        high = squares.astype(BF16).astype(F32)
        low = squares - high
        lane = lax.broadcasted_iota(jnp.int32, (128, 256), 1)
        for xx in range(NX):
            piece = acc[:, xx * 256 : (xx + 1) * 256]
            piece = jnp.where(lane == 192, high, jnp.where(lane == 193, low, piece))
            snd[k, xx] = piece.astype(BF16)
        for o in (2, 1, 3):
            part_x(k, o).start()

    def combine_step(k):
        total = snd[k, x].astype(F32)
        for o in (1, 2, 3):
            part_x(k, o).wait_recv()
            total += part[o - 1, k].astype(F32)
        lane = lax.broadcasted_iota(jnp.int32, (128, 256), 1)
        squares = jnp.sum(jnp.where((lane == 192) | (lane == 193), total, 0.0), axis=1, keepdims=True)
        out = (total * lax.rsqrt(squares / (NX * 2 * HALF) + 1e-6) + bias[...]).astype(BF16)
        for side in range(2):
            zz = (z + NZ - k) % NZ if side == 0 else (z + k) % NZ
            for i in range(2):
                xt = 2 * side + i
                rows = out[xt * 32 : (xt + 1) * 32]
                q_out[xt, zz] = rows[:, :128]
                kv_out[0, xt, zz] = rows[:, 128:160]
                kv_out[1, xt, zz] = rows[:, 160:192]

    for u in range(NZ):
        for copy in hid_local(u):
            copy.start()
    for r in range(2):
        w_local(r).start()
    res_local().start()
    wq_local().start()
    rsb[0, 0] = jnp.zeros(rsb.shape[2:], BF16)
    rsb[1, 0] = jnp.zeros(rsb.shape[2:], BF16)

    barrier = pltpu.get_barrier_semaphore()
    friends = [to_x(1), to_x(2), to_x(3), to_z(1), to_z(-1), to_y(1), to_y(2), to_y(3), sibling]
    for friend in friends:
        pl.semaphore_signal(barrier, inc=1, device_id=friend, device_id_type=MESH)
    pl.semaphore_wait(barrier, len(friends))

    for o in (2, 1, 3):
        w_x(0, o).start()
    for u in range(3):
        own_send(u)
    w_spread_y(0)
    front(0)
    own_send(3)
    front(1)
    own_send(4)
    w_spread_c(0)
    front(2)
    own_send(5)
    w_ready(0)

    @pl.loop(0, NZ)
    def _(k):
        @pl.when(k + AHEAD < NZ)
        def _():
            front(k + AHEAD)

        @pl.when(k + 6 < NZ)
        def _():
            own_send(k + 6)

        @pl.when(k == 1)
        def _():
            for o in (2, 1, 3):
                w_x(1, o).start()

        @pl.when(k == 3)
        def _():
            w_spread_y(1)
            for o in (2, 1, 3):
                res_x(o).start()

        @pl.when(k == 4)
        def _():
            for o in (2, 1, 3):
                q_x(o).start()

        @pl.when(k == 6)
        def _():
            w_spread_c(1)

        @pl.when(k == 7)
        def _():
            res_local().wait()
            for o in (2, 1, 3):
                res_x_in(o).wait_recv()

        back(k)
        reduce_step(0, k)

    residual_out(0)
    w_ready(1)

    @pl.loop(0, NZ)
    def _(k):
        @pl.when(k == 0)
        def _():
            wq_local().wait()
            for o in (1, 3, 2):
                q_x_in(o).wait_recv()
            for p in (1, 3, 2):
                q_y(p).start()

        @pl.when(k == 5)
        def _():
            for p in (1, 3, 2):
                q_y_in(p).wait_recv()
            q_c().start()

        reduce_step(1, k)
        gather_step(0, k)

    residual_out(1)
    q_c_in().wait_recv()

    @pl.loop(0, NZ)
    def _(k):
        gather_step(1, k)
        project_step(k)

        @pl.when(k >= 3)
        def _():
            combine_step(k - 3)

    @pl.loop(NZ - 3, NZ)
    def _(k):
        combine_step(k)

    for r in range(2):
        nr_local(r).wait()
        for o in (1, 2, 3):
            nr_x_in(r, o).wait_recv()
            nr_x(r, o).wait_send()
            w_x(r, o).wait_send()
            w_c(r, o).wait_send()
            for p in (1, 2, 3):
                w_y(r, o, p).wait_send()
    for o in (1, 2, 3):
        q_x(o).wait_send()
        q_y(o).wait_send()
        res_x(o).wait_send()
    q_c().wait_send()

    @pl.loop(0, NZ)
    def _(k):
        for side in range(2):
            h_direct(k, side).wait_send()
            h_forward(k, side).wait_send()
        for o in (1, 2, 3):
            part_x(k, o).wait_send()

    @pl.loop(0, NZ - 1)
    def _(k):
        for r in range(2):
            for side in range(2):
                for j in range(2):
                    ring(rsb, rs_s, rs_r, r, k, side, j).wait_send()
                    ring(yb, ag_s, ag_r, r, k, side, j).wait_send()


def per_device(
    hidden,
    residual,
    down_weight,
    norm_gain,
    query_codes,
    query_scales,
    pair_codes,
    pair_scales,
    input_groups,
    query_bias,
    pair_bias,
):
    d = lax.axis_index("dp")
    rank = (d % NC) * NY + d // NC
    group_count = query_scales.shape[0]

    def share(a):
        return lax.dynamic_index_in_dim(a.reshape((NX, 2, 8, 128) + a.shape[1:]), rank, 2, keepdims=False)

    codes = jnp.concatenate([share(query_codes), share(pair_codes[0]), share(pair_codes[1])], axis=-1)
    scales = jnp.concatenate([query_scales, pair_scales[0], pair_scales[1]], axis=-1)
    selector = (share(input_groups)[..., None] == jnp.arange(group_count, dtype=jnp.int32)).astype(BF16)
    scale_rows = jnp.dot(selector.reshape(1024, group_count), scales, preferred_element_type=F32)
    scale_rows = scale_rows.reshape(codes.shape)
    gain = share(norm_gain).astype(F32)[..., None]
    wq = (codes.astype(F32) * scale_rows * gain).astype(BF16)
    wq = jnp.pad(wq, ((0, 0), (0, 0), (0, 0), (0, 64)))
    bias = jnp.concatenate([query_bias, pair_bias[0], pair_bias[1], jnp.zeros((64,), BF16)]).astype(F32)[None]
    depth = hidden.shape[1]
    dma = pltpu.SemaphoreType.DMA
    pairs = []
    for shape in (
        (8, 4), (2, 3), (2, 3, 3), (2, 3), (3,), (3,), (1,),
        (3,), (2, 7, 2, 2), (2, 7, 2, 2), (2, 3), (8, 3),
    ):
        pairs += [dma(shape), dma(shape)]
    new_residual, queries, key_values = pl.pallas_call(
        kernel,
        out_shape=(
            jax.ShapeDtypeStruct(residual.shape, BF16),
            jax.ShapeDtypeStruct((4, 8, 32, 128), BF16),
            jax.ShapeDtypeStruct((2, 4, 8, 32, 32), BF16),
        ),
        in_specs=[pl.BlockSpec(memory_space=pl.ANY)] * 4 + [pl.BlockSpec(memory_space=pltpu.VMEM)],
        out_specs=(
            pl.BlockSpec(memory_space=pl.ANY),
            pl.BlockSpec(memory_space=pltpu.VMEM),
            pl.BlockSpec(memory_space=pltpu.VMEM),
        ),
        scratch_shapes=[
            pltpu.VMEM((2, NX, depth, HALF), BF16),
            pltpu.VMEM((NX, NZ, 4, 32, depth), BF16),
            pltpu.VMEM((2, NZ, 4, 32, HALF), BF16),
            pltpu.VMEM((2, NZ, 4, 32, HALF), BF16),
            pltpu.VMEM((2, HALF, NX * 256), BF16),
            pltpu.VMEM((3, NZ, 128, 256), BF16),
            pltpu.VMEM((NZ, NX, 128, 256), BF16),
            pltpu.VMEM((4, 32, 2 * HALF), BF16),
            dma((8, 2)), dma((2,)), dma((1,)), dma((1,)), dma((2,)),
        ] + pairs,
        compiler_params=pltpu.CompilerParams(
            collective_id=0, has_side_effects=True, vmem_limit_bytes=58 * 2**20
        ),
        cost_estimate=pl.CostEstimate(flops=12_000_000_000, bytes_accessed=14_000_000, transcendentals=0),
    )(hidden.reshape(4, 8, 32, depth), residual, down_weight, wq, bias)
    return new_residual, queries.reshape(1024, 128), key_values.reshape(2, 1024, 32)


def solution(mesh):
    in_specs = (
        P("dp", "tensor"),
        P(("dp", "tensor"), None),
        P("tensor", None),
        P(),
        P(None, "tensor"),
        P(None, "tensor"),
        P(None, None, "tensor"),
        P(None, None, "tensor"),
        P(),
        P("tensor"),
        P(None, "tensor"),
    )
    out_specs = (P(("dp", "tensor"), None), P("dp", "tensor"), P(None, "dp", "tensor"))
    return jax.shard_map(
        per_device, mesh=mesh, in_specs=in_specs, out_specs=out_specs, check_vma=False
    )
```

```python
import jax
import jax.numpy as jnp
from jax import lax
from jax.experimental import pallas as pl
from jax.experimental.pallas import tpu as pltpu
from jax.sharding import PartitionSpec as P

MESH = pl.DeviceIdType.MESH
NX, NZ, NY, NC = 4, 8, 4, 2
F32, BF16 = jnp.float32, jnp.bfloat16
NQ, QW = 4, 512
XW = NQ * QW


def kernel(
    hid, res, w, wq, bias, nr_out, q_out, kv_out,
    wb, hb, rsb, yb, wqp, kvw, part, snd, resb,
    l_h, l_w, l_r, l_q, l_n,
    h_s, h_r, w_s, w_r, wy_s, wy_r, wc_s, wc_r, q_s, q_r, qy_s, qy_r, qc_s, qc_r,
    r_s, r_r, rs_s, rs_r, ag_s, ag_r, n_s, n_r, p_s, p_r,
):
    t, d = lax.axis_index("tensor"), lax.axis_index("dp")
    x, z = t // NZ, t % NZ
    y, c = d // NC, d % NC
    depth = hid.shape[-1]
    half = depth // 2
    cut = half // 32 * 16 + 16

    def at(xx, zz, yy, cc):
        return {"tensor": xx * NZ + zz, "dp": yy * NC + cc}

    def to_x(o):
        return at((x + o) % NX, z, y, c)

    def to_z(o):
        return at(x, (z + o + NZ) % NZ, y, c)

    def to_y(o):
        return at(x, z, (y + o) % NY, c)

    sibling = at(x, z, y, 1 - c)

    def remote(src, dst, ss, rs, device):
        return pltpu.make_async_remote_copy(
            src_ref=src, dst_ref=dst, send_sem=ss, recv_sem=rs, device_id=device, device_id_type=MESH
        )

    def xs(o):
        return (x + o) % NX

    def ys(o):
        return (y + o) % NY

    step_of = (1, 3)

    def hid_local(u):
        zl, zh = (z + 2 * NZ - 1 - u) % NZ, (z + 1 + u) % NZ
        return (
            pltpu.make_async_copy(hid.at[pl.ds(0, 2), zl], hb.at[0, u, pl.ds(0, 2)], l_h.at[u, 0]),
            pltpu.make_async_copy(hid.at[pl.ds(2, 2), zh], hb.at[0, u, pl.ds(2, 2)], l_h.at[u, 1]),
        )

    def w_local(q, i):
        return pltpu.make_async_copy(
            w.at[:, pl.ds(x * XW + q * QW + i * 128, 128)], wb.at[q, 0, i], l_w.at[q, i]
        )

    def res_local():
        return pltpu.make_async_copy(res.at[:, pl.ds(x * XW, XW)], resb.at[x], l_r.at[0])

    rank = c * NY + y

    def wq_local():
        return pltpu.make_async_copy(wq.at[x], wqp.at[0, rank], l_q.at[0])

    def nr_local(q):
        return pltpu.make_async_copy(
            yb.at[q, 0, x], nr_out.at[:, pl.ds(x * XW + q * QW, QW)], l_n.at[q]
        )

    def h_direct(u, side):
        return remote(
            hb.at[0, u], hb.at[NX - step_of[side], u], h_s.at[u, side], h_r.at[u, side], to_x(step_of[side])
        )

    def h_direct_in(u, side):
        ref = hb.at[NX - step_of[side], u]
        return remote(ref, ref, h_s.at[u, side], h_r.at[u, side], to_x(step_of[side]))

    def h_forward(u, side):
        rows = pl.ds(2 * side, 2)
        return remote(
            hb.at[NX - step_of[side], u, rows], hb.at[2, u, rows],
            h_s.at[u, 2 + side], h_r.at[u, 2 + side], to_x(step_of[side]),
        )

    def h_forward_in(u, side):
        ref = hb.at[2, u, pl.ds(2 * side, 2)]
        return remote(ref, ref, h_s.at[u, 2 + side], h_r.at[u, 2 + side], to_x(step_of[side]))

    def w_x(q, o):
        cols = pl.ds(xs(o) * XW + q * QW + y * 128, 128)
        rows = pl.ds(c * half, half)
        return remote(
            w.at[rows, cols], wb.at[q, NX - o, y, rows], w_s.at[q, o - 1], w_r.at[q, o - 1], to_x(o)
        )

    def w_x_in(q, o):
        ref = wb.at[q, NX - o, y, pl.ds(c * half, half)]
        return remote(ref, ref, w_s.at[q, o - 1], w_r.at[q, o - 1], to_x(o))

    def w_y(q, side):
        ref = wb.at[q, pl.ds(1, NX - 1), y, pl.ds(c * half, half)]
        return remote(ref, ref, wy_s.at[q, side], wy_r.at[q, side], to_y(step_of[side]))

    def w_y_in(q, side):
        ref = wb.at[q, pl.ds(1, NX - 1), ys(NY - step_of[side]), pl.ds(c * half, half)]
        return remote(ref, ref, wy_s.at[q, side], wy_r.at[q, side], to_y(step_of[side]))

    def w_part(q, yy, side):
        rows = pl.ds(c * half, cut) if side == 0 else pl.ds(c * half + cut, half - cut)
        return wb.at[q, pl.ds(1, NX - 1), yy, rows]

    def w_forward(q, side):
        ref = w_part(q, ys(NY - step_of[side]), side)
        return remote(ref, ref, wy_s.at[q, 2 + side], wy_r.at[q, 2 + side], to_y(step_of[side]))

    def w_forward_in(q, side):
        ref = w_part(q, ys(2), side)
        return remote(ref, ref, wy_s.at[q, 2 + side], wy_r.at[q, 2 + side], to_y(step_of[side]))

    def w_c(q):
        ref = wb.at[q, pl.ds(1, NX - 1), :, pl.ds(c * half, half)]
        return remote(ref, ref, wc_s.at[q], wc_r.at[q], sibling)

    def w_c_in(q):
        ref = wb.at[q, pl.ds(1, NX - 1), :, pl.ds((1 - c) * half, half)]
        return remote(ref, ref, wc_s.at[q], wc_r.at[q], sibling)

    def q_x(o):
        return remote(wq.at[xs(o)], wqp.at[NX - o, rank], q_s.at[o - 1], q_r.at[o - 1], to_x(o))

    def q_x_in(o):
        ref = wqp.at[NX - o, rank]
        return remote(ref, ref, q_s.at[o - 1], q_r.at[o - 1], to_x(o))

    def q_y(side):
        ref = wqp.at[:, rank]
        return remote(ref, ref, qy_s.at[side], qy_r.at[side], to_y(step_of[side]))

    def q_y_in(side):
        ref = wqp.at[:, c * NY + ys(NY - step_of[side])]
        return remote(ref, ref, qy_s.at[side], qy_r.at[side], to_y(step_of[side]))

    def q_forward(side):
        ref = wqp.at[:, c * NY + ys(NY - step_of[side]), pl.ds(192 * side, 192)]
        return remote(ref, ref, qy_s.at[2 + side], qy_r.at[2 + side], to_y(step_of[side]))

    def q_forward_in(side):
        ref = wqp.at[:, c * NY + ys(2), pl.ds(192 * side, 192)]
        return remote(ref, ref, qy_s.at[2 + side], qy_r.at[2 + side], to_y(step_of[side]))

    def q_c():
        ref = wqp.at[:, pl.ds(c * NY, NY)]
        return remote(ref, ref, qc_s.at[0], qc_r.at[0], sibling)

    def q_c_in():
        ref = wqp.at[:, pl.ds((1 - c) * NY, NY)]
        return remote(ref, ref, qc_s.at[0], qc_r.at[0], sibling)

    def res_x(o):
        return remote(
            res.at[:, pl.ds(xs(o) * XW, XW)], resb.at[x], r_s.at[o - 1], r_r.at[o - 1], to_x(o)
        )

    def res_x_in(o):
        ref = resb.at[xs(NX - o)]
        return remote(ref, ref, r_s.at[o - 1], r_r.at[o - 1], to_x(o))

    def ring(buf, ss, rs, q, k, side):
        rows = pl.ds(2 * side, 2)
        return remote(
            buf.at[q, k, rows], buf.at[q, k + 1, rows],
            ss.at[q, k, side], rs.at[q, k, side], to_z(1 if side == 0 else -1),
        )

    def ring_in(buf, ss, rs, q, k, side):
        ref = buf.at[q, k, pl.ds(2 * side, 2)]
        return remote(ref, ref, ss.at[q, k - 1, side], rs.at[q, k - 1, side], to_z(1))

    def nr_x(q, o):
        return remote(
            yb.at[q, 0, xs(o)], nr_out.at[:, pl.ds(x * XW + q * QW, QW)],
            n_s.at[q, o - 1], n_r.at[q, o - 1], to_x(o),
        )

    def nr_x_in(q, o):
        ref = nr_out.at[:, pl.ds(xs(NX - o) * XW + q * QW, QW)]
        return remote(ref, ref, n_s.at[q, o - 1], n_r.at[q, o - 1], to_x(o))

    def part_x(k, o):
        return remote(snd.at[k, o], part.at[o - 1, k], p_s.at[k, o - 1], p_r.at[k, o - 1], to_x(o))

    others = (2, 1, 3)

    def h_send(u):
        for copy in hid_local(u):
            copy.wait()
        for side in range(2):
            h_direct(u, side).start()

    def h_pass(u):
        for side in range(2):
            h_direct_in(u, side).wait_recv()
            h_forward(u, side).start()

    def h_ready(u):
        for side in range(2):
            h_forward_in(u, side).wait_recv()

    def w_send(q):
        for o in others:
            w_x(q, o).start()

    def w_spread(q):
        for o in (1, 3, 2):
            w_x_in(q, o).wait_recv()
        for side in range(2):
            w_y(q, side).start()

    def w_pass(q):
        for side in range(2):
            w_y_in(q, side).wait_recv()
            w_forward(q, side).start()

    def w_share(q):
        for side in range(2):
            w_forward_in(q, side).wait_recv()
        w_c(q).start()

    def w_ready(q):
        for i in range(4):
            w_local(q, i).wait()
        w_c_in(q).wait_recv()

    def reduce_step(q, k):
        acc = jnp.zeros((128, QW), F32)
        for o in range(NX):
            weight = jnp.concatenate([wb[q, o, i] for i in range(4)], axis=1)
            acc += jnp.dot(hb[o, k].reshape(128, depth), weight, preferred_element_type=F32)

        @pl.when(k > 0)
        def _():
            for side in range(2):
                ring_in(rsb, rs_s, rs_r, q, k, side).wait_recv()

        acc += rsb[q, k].reshape(128, QW).astype(F32)

        @pl.when(k < NZ - 1)
        def _():
            rsb[q, k] = acc.astype(BF16).reshape(4, 32, QW)
            for side in range(2):
                ring(rsb, rs_s, rs_r, q, k, side).start()

        @pl.when(k == NZ - 1)
        def _():
            own = resb[:, :, pl.ds(pl.multiple_of(q * QW, QW), QW)].reshape(128, QW).astype(F32)
            yb[q, 0] = (acc + own).astype(BF16).reshape(4, 32, QW)
            for side in range(2):
                ring(yb, ag_s, ag_r, q, 0, side).start()
            nr_local(q).start()
            for o in others:
                nr_x(q, o).start()

    def gather_step(q, k):
        for side in range(2):
            ring_in(yb, ag_s, ag_r, q, k, side).wait_recv()

        @pl.when(k < NZ - 1)
        def _():
            for side in range(2):
                ring(yb, ag_s, ag_r, q, k, side).start()

    def project_step(k):
        acc_q = [jnp.zeros((128, 256), F32), jnp.zeros((128, 256), F32)]
        acc_kv = jnp.zeros((128, 256), F32)
        squares = jnp.zeros((128, 1), F32)
        for q in range(NQ):
            rows = yb[q, k].reshape(128, QW)
            for pair in range(2):
                weight = jnp.concatenate(
                    [
                        jnp.concatenate([wqp[2 * pair + i, 2 * q + j, 0:256] for j in range(2)], axis=0)
                        for i in range(2)
                    ],
                    axis=1,
                )
                acc_q[pair] += jnp.dot(rows, weight, preferred_element_type=F32)
            acc_kv += jnp.dot(rows, kvw[q * QW : (q + 1) * QW], preferred_element_type=F32)
            wide = rows.astype(F32)
            squares += jnp.sum(wide * wide, axis=1, keepdims=True)
        high = squares.astype(BF16).astype(F32)
        low = squares - high
        lane = lax.broadcasted_iota(jnp.int32, (128, 64), 1)
        extra = jnp.where(lane == 0, high, jnp.where(lane == 1, low, 0.0))
        for o in range(NX):
            snd[k, o, :, 0:128] = acc_q[o // 2][:, (o % 2) * 128 : (o % 2 + 1) * 128].astype(BF16)
            snd[k, o, :, 128:256] = jnp.concatenate(
                [acc_kv[:, o * 64 : (o + 1) * 64], extra], axis=1
            ).astype(BF16)
        for o in others:
            part_x(k, o).start()

    def combine_step(k):
        total = snd[k, 0].astype(F32)
        for o in (1, 2, 3):
            part_x(k, o).wait_recv()
            total += part[o - 1, k].astype(F32)
        lane = lax.broadcasted_iota(jnp.int32, (128, 256), 1)
        squares = jnp.sum(jnp.where((lane == 192) | (lane == 193), total, 0.0), axis=1, keepdims=True)
        out = (total * lax.rsqrt(squares / (NX * XW) + 1e-6) + bias[...]).astype(BF16)
        for side in range(2):
            zz = (z + NZ - k) % NZ if side == 0 else (z + k) % NZ
            for i in range(2):
                xt = 2 * side + i
                rows = out[xt * 32 : (xt + 1) * 32]
                q_out[xt, zz] = rows[:, :128]
                kv_out[0, xt, zz] = rows[:, 128:160]
                kv_out[1, xt, zz] = rows[:, 160:192]

    for u in range(NZ):
        for copy in hid_local(u):
            copy.start()
    for q in range(NQ):
        for i in range(4):
            w_local(q, i).start()
    res_local().start()
    wq_local().start()
    for q in range(NQ):
        rsb[q, 0] = jnp.zeros(rsb.shape[2:], BF16)

    barrier = pltpu.get_barrier_semaphore()
    friends = [to_x(1), to_x(2), to_x(3), to_z(1), to_z(-1), to_y(1), to_y(3), sibling]
    for friend in friends:
        pl.semaphore_signal(barrier, inc=1, device_id=friend, device_id_type=MESH)
    pl.semaphore_wait(barrier, len(friends))

    w_send(0)
    h_send(0)
    w_spread(0)
    w_send(1)
    w_send(2)
    h_pass(0)
    h_send(1)
    w_pass(0)
    w_spread(1)
    w_send(3)
    w_spread(2)
    w_share(0)
    h_pass(1)
    h_send(2)
    w_ready(0)
    w_pass(1)
    w_spread(3)

    @pl.loop(0, NZ)
    def _(s):
        h_ready(s)

        @pl.when(s == NZ - 1)
        def _():
            res_local().wait()
            for o in others:
                res_x_in(o).wait_recv()

        @pl.loop(0, NQ)
        def _(q):
            @pl.when((q == s) & (s > 0))
            def _():
                w_share(q)
                w_ready(q)

            @pl.when(q <= s)
            def _():
                reduce_step(q, jnp.where(s > 2 * q, s, jnp.maximum(2 * (s - q) - 1, 0)))

        @pl.loop(1, NQ)
        def _(q):
            @pl.when((q < s) & (s <= 2 * q))
            def _():
                reduce_step(q, 2 * (s - q))

        @pl.when(s < NQ - 2)
        def _():
            w_pass(s + 2)

        @pl.when(s < NZ - 2)
        def _():
            h_pass(s + 2)

        @pl.when(s < NZ - 3)
        def _():
            h_send(s + 3)

        @pl.when(s == 3)
        def _():
            for o in others:
                q_x(o).start()

        @pl.when(s == 4)
        def _():
            for o in others:
                res_x(o).start()
            wq_local().wait()
            for o in (1, 3, 2):
                q_x_in(o).wait_recv()
            for side in range(2):
                q_y(side).start()

        @pl.when(s == 5)
        def _():
            for side in range(2):
                q_y_in(side).wait_recv()
                q_forward(side).start()

        @pl.when(s == 6)
        def _():
            for side in range(2):
                q_forward_in(side).wait_recv()
            q_c().start()

    q_c_in().wait_recv()
    for i in range(2 * NY):
        packed = [wqp[o, i, 256:384] for o in range(NX)]
        for j in range(2):
            kvw[i * 256 + j * 128 : i * 256 + (j + 1) * 128] = jnp.concatenate(
                [p[:, j * 64 : (j + 1) * 64] for p in packed], axis=1
            )

    @pl.loop(0, NZ)
    def _(k):
        @pl.when(k > 0)
        def _():
            @pl.loop(0, NQ)
            def _(q):
                gather_step(q, k)

        project_step(k)

        @pl.when(k >= 2)
        def _():
            combine_step(k - 2)

    @pl.loop(NZ - 2, NZ)
    def _(k):
        combine_step(k)

    @pl.loop(0, NQ)
    def _(q):
        nr_local(q).wait()
        for o in (1, 2, 3):
            nr_x_in(q, o).wait_recv()
            nr_x(q, o).wait_send()
            w_x(q, o).wait_send()
        for side in range(2):
            w_y(q, side).wait_send()
            w_forward(q, side).wait_send()
        w_c(q).wait_send()

    for o in (1, 2, 3):
        q_x(o).wait_send()
        res_x(o).wait_send()
    for side in range(2):
        q_y(side).wait_send()
        q_forward(side).wait_send()
    q_c().wait_send()

    @pl.loop(0, NZ)
    def _(k):
        for side in range(2):
            h_direct(k, side).wait_send()
            h_forward(k, side).wait_send()
        for o in (1, 2, 3):
            part_x(k, o).wait_send()

    @pl.loop(0, NZ - 1)
    def _(k):
        for q in range(NQ):
            for side in range(2):
                ring(rsb, rs_s, rs_r, q, k, side).wait_send()
                ring(yb, ag_s, ag_r, q, k, side).wait_send()


def per_device(
    hidden,
    residual,
    down_weight,
    norm_gain,
    query_codes,
    query_scales,
    pair_codes,
    pair_scales,
    input_groups,
    query_bias,
    pair_bias,
):
    d = lax.axis_index("dp")
    rank = (d % NC) * NY + d // NC
    group_count = query_scales.shape[0]

    def share(a):
        return lax.dynamic_index_in_dim(a.reshape((NX, 8, 256) + a.shape[1:]), rank, 1, keepdims=False)

    codes = jnp.concatenate([share(query_codes), share(pair_codes[0]), share(pair_codes[1])], axis=-1)
    scales = jnp.concatenate([query_scales, pair_scales[0], pair_scales[1]], axis=-1)
    selector = (share(input_groups)[..., None] == jnp.arange(group_count, dtype=jnp.int32)).astype(BF16)
    scale_rows = jnp.dot(selector.reshape(1024, group_count), scales, preferred_element_type=F32)
    scale_rows = scale_rows.reshape(codes.shape)
    gain = share(norm_gain).astype(F32)[..., None]
    wq = (codes.astype(F32) * scale_rows * gain).astype(BF16)
    kv = jnp.concatenate([wq[:, :128, 128:], wq[:, 128:, 128:]], axis=-1)
    wq = jnp.concatenate([wq[:, :, :128], kv], axis=1)
    bias = jnp.concatenate([query_bias, pair_bias[0], pair_bias[1], jnp.zeros((64,), BF16)]).astype(F32)[None]
    depth = hidden.shape[1]
    dma = pltpu.SemaphoreType.DMA
    pairs = []
    for shape in (
        (8, 4), (NQ, 3), (NQ, 4), (NQ,), (3,), (4,), (1,),
        (3,), (NQ, 7, 2), (NQ, 7, 2), (NQ, 3), (8, 3),
    ):
        pairs += [dma(shape), dma(shape)]
    new_residual, queries, key_values = pl.pallas_call(
        kernel,
        out_shape=(
            jax.ShapeDtypeStruct(residual.shape, BF16),
            jax.ShapeDtypeStruct((4, 8, 32, 128), BF16),
            jax.ShapeDtypeStruct((2, 4, 8, 32, 32), BF16),
        ),
        in_specs=[pl.BlockSpec(memory_space=pl.ANY)] * 4 + [pl.BlockSpec(memory_space=pltpu.VMEM)],
        out_specs=(
            pl.BlockSpec(memory_space=pl.ANY),
            pl.BlockSpec(memory_space=pltpu.VMEM),
            pl.BlockSpec(memory_space=pltpu.VMEM),
        ),
        scratch_shapes=[
            pltpu.VMEM((NQ, NX, 4, depth, 128), BF16),
            pltpu.VMEM((NX, NZ, 4, 32, depth), BF16),
            pltpu.VMEM((NQ, NZ, 4, 32, QW), BF16),
            pltpu.VMEM((NQ, NZ, 4, 32, QW), BF16),
            pltpu.VMEM((NX, 8, 384, 128), BF16),
            pltpu.VMEM((XW, 256), BF16),
            pltpu.VMEM((3, NZ, 128, 256), BF16),
            pltpu.VMEM((NZ, NX, 128, 256), BF16),
            pltpu.VMEM((4, 32, XW), BF16),
            dma((8, 2)), dma((NQ, 4)), dma((1,)), dma((1,)), dma((NQ,)),
        ] + pairs,
        compiler_params=pltpu.CompilerParams(
            collective_id=0, has_side_effects=True, vmem_limit_bytes=58 * 2**20
        ),
        cost_estimate=pl.CostEstimate(flops=12_000_000_000, bytes_accessed=14_000_000, transcendentals=0),
    )(hidden.reshape(4, 8, 32, depth), residual, down_weight, wq, bias)
    return new_residual, queries.reshape(1024, 128), key_values.reshape(2, 1024, 32)


def solution(mesh):
    in_specs = (
        P("dp", "tensor"),
        P(("dp", "tensor"), None),
        P("tensor", None),
        P(),
        P(None, "tensor"),
        P(None, "tensor"),
        P(None, None, "tensor"),
        P(None, None, "tensor"),
        P(),
        P("tensor"),
        P(None, "tensor"),
    )
    out_specs = (P(("dp", "tensor"), None), P("dp", "tensor"), P(None, "dp", "tensor"))
    return jax.shard_map(
        per_device, mesh=mesh, in_specs=in_specs, out_specs=out_specs, check_vma=False
    )
```

```python
import jax
import jax.numpy as jnp
from jax import lax
from jax.experimental import pallas as pl
from jax.experimental.pallas import tpu as pltpu
from jax.sharding import PartitionSpec as P

MESH = pl.DeviceIdType.MESH
NX, NZ, NY, NC = 4, 8, 4, 2
F32, BF16 = jnp.float32, jnp.bfloat16
NQ, QW = 4, 512
XW = NQ * QW


def kernel(
    hid, res, w, qcodes, pcodes, groups, gains, qscales, pscales, qbias, pbias, nr_out, q_out, kv_out,
    wb, hb, rsb, yb, wq, qc, pc, wqp, kvw, part, snd, resb, gainf, ht,
    l_h, l_w, l_r, l_q, l_n, l_c,
    h_s, h_r, w_s, w_r, wy_s, wy_r, wc_s, wc_r, q_s, q_r, qy_s, qy_r, qc_s, qc_r,
    r_s, r_r, rs_s, rs_r, ag_s, ag_r, n_s, n_r, p_s, p_r,
):
    t, d = lax.axis_index("tensor"), lax.axis_index("dp")
    x, z = t // NZ, t % NZ
    y, c = d // NC, d % NC
    depth = hid.shape[0]
    half = depth // 2
    cut = half // 32 * 16 + 16

    def at(xx, zz, yy, cc):
        return {"tensor": xx * NZ + zz, "dp": yy * NC + cc}

    def to_x(o):
        return at((x + o) % NX, z, y, c)

    def to_z(o):
        return at(x, (z + o + NZ) % NZ, y, c)

    def to_y(o):
        return at(x, z, (y + o) % NY, c)

    sibling = at(x, z, y, 1 - c)

    def remote(src, dst, ss, rs, device):
        return pltpu.make_async_remote_copy(
            src_ref=src, dst_ref=dst, send_sem=ss, recv_sem=rs, device_id=device, device_id_type=MESH
        )

    def xs(o):
        return (x + o) % NX

    def ys(o):
        return (y + o) % NY

    step_of = (1, 3)

    def hid_local():
        return pltpu.make_async_copy(hid, ht, l_h.at[0])

    def w_local(q, i):
        return pltpu.make_async_copy(
            w.at[:, pl.ds(x * XW + q * QW + i * 128, 128)], wb.at[q, 0, i], l_w.at[q, i]
        )

    def res_local():
        return pltpu.make_async_copy(res.at[:, pl.ds(x * XW, XW)], resb.at[x], l_r.at[0])

    rank = c * NY + y

    def wq_local():
        return pltpu.make_async_copy(wq.at[x], wqp.at[0, rank], l_q.at[0])

    def codes_local(o):
        rows = pl.ds(pl.multiple_of(o * XW + rank * 256, 256), 256)
        return (
            pltpu.make_async_copy(qcodes.at[rows], qc.at[o], l_c.at[o, 0]),
            pltpu.make_async_copy(pcodes.at[:, :, rows], pc.at[o], l_c.at[o, 1]),
        )

    def nr_local(q):
        return pltpu.make_async_copy(
            yb.at[q, 0, x], nr_out.at[:, pl.ds(x * XW + q * QW, QW)], l_n.at[q]
        )

    def h_direct(u, side):
        return remote(
            hb.at[0, u], hb.at[NX - step_of[side], u], h_s.at[u, side], h_r.at[u, side], to_x(step_of[side])
        )

    def h_direct_in(u, side):
        ref = hb.at[NX - step_of[side], u]
        return remote(ref, ref, h_s.at[u, side], h_r.at[u, side], to_x(step_of[side]))

    def h_forward(u, side):
        rows = pl.ds(2 * side, 2)
        return remote(
            hb.at[NX - step_of[side], u, rows], hb.at[2, u, rows],
            h_s.at[u, 2 + side], h_r.at[u, 2 + side], to_x(step_of[side]),
        )

    def h_forward_in(u, side):
        ref = hb.at[2, u, pl.ds(2 * side, 2)]
        return remote(ref, ref, h_s.at[u, 2 + side], h_r.at[u, 2 + side], to_x(step_of[side]))

    def w_x(q, o):
        cols = pl.ds(xs(o) * XW + q * QW + y * 128, 128)
        rows = pl.ds(c * half, half)
        return remote(
            w.at[rows, cols], wb.at[q, NX - o, y, rows], w_s.at[q, o - 1], w_r.at[q, o - 1], to_x(o)
        )

    def w_x_in(q, o):
        ref = wb.at[q, NX - o, y, pl.ds(c * half, half)]
        return remote(ref, ref, w_s.at[q, o - 1], w_r.at[q, o - 1], to_x(o))

    def w_y(q, side):
        ref = wb.at[q, pl.ds(1, NX - 1), y, pl.ds(c * half, half)]
        return remote(ref, ref, wy_s.at[q, side], wy_r.at[q, side], to_y(step_of[side]))

    def w_y_in(q, side):
        ref = wb.at[q, pl.ds(1, NX - 1), ys(NY - step_of[side]), pl.ds(c * half, half)]
        return remote(ref, ref, wy_s.at[q, side], wy_r.at[q, side], to_y(step_of[side]))

    def w_part(q, yy, side):
        rows = pl.ds(c * half, cut) if side == 0 else pl.ds(c * half + cut, half - cut)
        return wb.at[q, pl.ds(1, NX - 1), yy, rows]

    def w_forward(q, side):
        ref = w_part(q, ys(NY - step_of[side]), side)
        return remote(ref, ref, wy_s.at[q, 2 + side], wy_r.at[q, 2 + side], to_y(step_of[side]))

    def w_forward_in(q, side):
        ref = w_part(q, ys(2), side)
        return remote(ref, ref, wy_s.at[q, 2 + side], wy_r.at[q, 2 + side], to_y(step_of[side]))

    def w_c(q):
        ref = wb.at[q, pl.ds(1, NX - 1), :, pl.ds(c * half, half)]
        return remote(ref, ref, wc_s.at[q], wc_r.at[q], sibling)

    def w_c_in(q):
        ref = wb.at[q, pl.ds(1, NX - 1), :, pl.ds((1 - c) * half, half)]
        return remote(ref, ref, wc_s.at[q], wc_r.at[q], sibling)

    def q_x(o):
        return remote(wq.at[xs(o)], wqp.at[NX - o, rank], q_s.at[o - 1], q_r.at[o - 1], to_x(o))

    def q_x_in(o):
        ref = wqp.at[NX - o, rank]
        return remote(ref, ref, q_s.at[o - 1], q_r.at[o - 1], to_x(o))

    def q_y(side):
        ref = wqp.at[:, rank]
        return remote(ref, ref, qy_s.at[side], qy_r.at[side], to_y(step_of[side]))

    def q_y_in(side):
        ref = wqp.at[:, c * NY + ys(NY - step_of[side])]
        return remote(ref, ref, qy_s.at[side], qy_r.at[side], to_y(step_of[side]))

    def q_forward(side):
        ref = wqp.at[:, c * NY + ys(NY - step_of[side]), pl.ds(192 * side, 192)]
        return remote(ref, ref, qy_s.at[2 + side], qy_r.at[2 + side], to_y(step_of[side]))

    def q_forward_in(side):
        ref = wqp.at[:, c * NY + ys(2), pl.ds(192 * side, 192)]
        return remote(ref, ref, qy_s.at[2 + side], qy_r.at[2 + side], to_y(step_of[side]))

    def q_c():
        ref = wqp.at[:, pl.ds(c * NY, NY)]
        return remote(ref, ref, qc_s.at[0], qc_r.at[0], sibling)

    def q_c_in():
        ref = wqp.at[:, pl.ds((1 - c) * NY, NY)]
        return remote(ref, ref, qc_s.at[0], qc_r.at[0], sibling)

    def res_x(o):
        return remote(
            res.at[:, pl.ds(xs(o) * XW, XW)], resb.at[x], r_s.at[o - 1], r_r.at[o - 1], to_x(o)
        )

    def res_x_in(o):
        ref = resb.at[xs(NX - o)]
        return remote(ref, ref, r_s.at[o - 1], r_r.at[o - 1], to_x(o))

    def ring(buf, ss, rs, q, k, side):
        rows = pl.ds(2 * side, 2)
        return remote(
            buf.at[q, k, rows], buf.at[q, k + 1, rows],
            ss.at[q, k, side], rs.at[q, k, side], to_z(1 if side == 0 else -1),
        )

    def ring_in(buf, ss, rs, q, k, side):
        ref = buf.at[q, k, pl.ds(2 * side, 2)]
        return remote(ref, ref, ss.at[q, k - 1, side], rs.at[q, k - 1, side], to_z(1))

    def nr_x(q, o):
        return remote(
            yb.at[q, 0, xs(o)], nr_out.at[:, pl.ds(x * XW + q * QW, QW)],
            n_s.at[q, o - 1], n_r.at[q, o - 1], to_x(o),
        )

    def nr_x_in(q, o):
        ref = nr_out.at[:, pl.ds(xs(NX - o) * XW + q * QW, QW)]
        return remote(ref, ref, n_s.at[q, o - 1], n_r.at[q, o - 1], to_x(o))

    def part_x(k, o):
        return remote(snd.at[k, o], part.at[o - 1, k], p_s.at[k, o - 1], p_r.at[k, o - 1], to_x(o))

    others = (2, 1, 3)

    def h_send(u):
        for side in range(2):
            h_direct(u, side).start()

    def turn_hidden():
        hid_local().wait()
        for b in range(8):
            turned = ht[:, b * 128 : (b + 1) * 128].astype(F32).T.astype(BF16)
            for i in range(4):
                xt, zc = b // 2, (b % 2) * 4 + i
                u = (z + 2 * NZ - 1 - zc) % NZ if xt < 2 else (zc + 2 * NZ - 1 - z) % NZ
                hb[0, u, xt] = turned[i * 32 : (i + 1) * 32]

    def h_pass(u):
        for side in range(2):
            h_direct_in(u, side).wait_recv()
            h_forward(u, side).start()

    def h_ready(u):
        for side in range(2):
            h_forward_in(u, side).wait_recv()

    def w_send(q):
        for o in others:
            w_x(q, o).start()

    def w_spread(q):
        for o in (1, 3, 2):
            w_x_in(q, o).wait_recv()
        for side in range(2):
            w_y(q, side).start()

    def w_pass(q):
        for side in range(2):
            w_y_in(q, side).wait_recv()
            w_forward(q, side).start()

    def w_share(q):
        for side in range(2):
            w_forward_in(q, side).wait_recv()
        w_c(q).start()

    def w_ready(q):
        for i in range(4):
            w_local(q, i).wait()
        w_c_in(q).wait_recv()

    def scale_weights():
        row = lax.broadcasted_iota(jnp.int32, (qscales.shape[0], 128), 0)
        gainf[...] = gains[...].astype(F32)
        for o in range(NX):
            for copy in codes_local(o):
                copy.wait()
            picked = []
            for j in range(2):
                line = pl.ds(o * (XW // 128) + rank * 2 + j, 1)
                picked.append(jnp.where(row == groups[line, :], gainf[line, :], 0.0).astype(BF16))
            picked = jnp.concatenate(picked, axis=1)
            factor = lax.dot_general(
                picked, qscales[...], (((0,), (0,)), ((), ())), preferred_element_type=F32
            )
            wq[o, 0:256] = (qc[o].astype(F32) * factor).astype(BF16)
            factor = jnp.dot(pscales[...].reshape(64, -1), picked, preferred_element_type=F32)
            flat = pc[o].reshape(64, 256).astype(F32) * factor
            packed = jnp.concatenate([flat[:, :128], flat[:, 128:]], axis=0)
            wq[o, 256:384] = packed.T.astype(BF16)
        wq_local().start()

    def reduce_step(q, k):
        acc = jnp.zeros((128, QW), F32)
        for o in range(NX):
            weight = jnp.concatenate([wb[q, o, i] for i in range(4)], axis=1)
            acc += jnp.dot(hb[o, k].reshape(128, depth), weight, preferred_element_type=F32)

        @pl.when(k > 0)
        def _():
            for side in range(2):
                ring_in(rsb, rs_s, rs_r, q, k, side).wait_recv()

        acc += rsb[q, k].reshape(128, QW).astype(F32)

        @pl.when(k < NZ - 1)
        def _():
            rsb[q, k] = acc.astype(BF16).reshape(4, 32, QW)
            for side in range(2):
                ring(rsb, rs_s, rs_r, q, k, side).start()

        @pl.when(k == NZ - 1)
        def _():
            own = resb[:, :, pl.ds(pl.multiple_of(q * QW, QW), QW)].reshape(128, QW).astype(F32)
            yb[q, 0] = (acc + own).astype(BF16).reshape(4, 32, QW)
            for side in range(2):
                ring(yb, ag_s, ag_r, q, 0, side).start()
            nr_local(q).start()
            for o in others:
                nr_x(q, o).start()

    def gather_step(q, k):
        for side in range(2):
            ring_in(yb, ag_s, ag_r, q, k, side).wait_recv()

        @pl.when(k < NZ - 1)
        def _():
            for side in range(2):
                ring(yb, ag_s, ag_r, q, k, side).start()

    def project_step(k):
        acc_q = [jnp.zeros((128, 256), F32), jnp.zeros((128, 256), F32)]
        acc_kv = jnp.zeros((128, 256), F32)
        squares = jnp.zeros((128, 1), F32)
        for q in range(NQ):
            rows = yb[q, k].reshape(128, QW)
            for pair in range(2):
                weight = jnp.concatenate(
                    [
                        jnp.concatenate([wqp[2 * pair + i, 2 * q + j, 0:256] for j in range(2)], axis=0)
                        for i in range(2)
                    ],
                    axis=1,
                )
                acc_q[pair] += jnp.dot(rows, weight, preferred_element_type=F32)
            acc_kv += jnp.dot(rows, kvw[q * QW : (q + 1) * QW], preferred_element_type=F32)
            wide = rows.astype(F32)
            squares += jnp.sum(wide * wide, axis=1, keepdims=True)
        high = squares.astype(BF16).astype(F32)
        low = squares - high
        lane = lax.broadcasted_iota(jnp.int32, (128, 64), 1)
        extra = jnp.where(lane == 0, high, jnp.where(lane == 1, low, 0.0))
        for o in range(NX):
            snd[k, o, :, 0:128] = acc_q[o // 2][:, (o % 2) * 128 : (o % 2 + 1) * 128].astype(BF16)
            snd[k, o, :, 128:256] = jnp.concatenate(
                [acc_kv[:, o * 64 : (o + 1) * 64], extra], axis=1
            ).astype(BF16)
        for o in others:
            part_x(k, o).start()

    def combine_step(k):
        total = snd[k, 0].astype(F32)
        for o in (1, 2, 3):
            part_x(k, o).wait_recv()
            total += part[o - 1, k].astype(F32)
        lane = lax.broadcasted_iota(jnp.int32, (128, 256), 1)
        squares = jnp.sum(jnp.where((lane == 192) | (lane == 193), total, 0.0), axis=1, keepdims=True)
        out = total * lax.rsqrt(squares / (NX * XW) + 1e-6)
        wide_q = (out[:, :128] + qbias[...].astype(F32)).astype(BF16)
        wide_k = (out[:, 128:160] + pbias[0:1, :].astype(F32)).astype(BF16)
        wide_v = (out[:, 160:192] + pbias[1:2, :].astype(F32)).astype(BF16)
        for side in range(2):
            zz = (z + NZ - k) % NZ if side == 0 else (z + k) % NZ
            for i in range(2):
                xt = 2 * side + i
                rows = slice(xt * 32, (xt + 1) * 32)
                q_out[xt, zz] = wide_q[rows]
                kv_out[0, xt, zz] = wide_k[rows]
                kv_out[1, xt, zz] = wide_v[rows]

    hid_local().start()
    for q in range(NQ):
        for i in range(4):
            w_local(q, i).start()
    res_local().start()
    for o in range(NX):
        for copy in codes_local(o):
            copy.start()
    for q in range(NQ):
        rsb[q, 0] = jnp.zeros(rsb.shape[2:], BF16)

    barrier = pltpu.get_barrier_semaphore()
    friends = [to_x(1), to_x(2), to_x(3), to_z(1), to_z(-1), to_y(1), to_y(3), sibling]
    for friend in friends:
        pl.semaphore_signal(barrier, inc=1, device_id=friend, device_id_type=MESH)
    pl.semaphore_wait(barrier, len(friends))

    w_send(0)
    turn_hidden()
    h_send(0)
    scale_weights()
    w_spread(0)
    w_send(1)
    w_send(2)
    h_pass(0)
    h_send(1)
    w_pass(0)
    w_spread(1)
    w_send(3)
    w_spread(2)
    w_share(0)
    h_pass(1)
    h_send(2)
    w_ready(0)
    w_pass(1)
    w_spread(3)

    @pl.loop(0, NZ)
    def _(s):
        h_ready(s)

        @pl.when(s == NZ - 1)
        def _():
            res_local().wait()
            for o in others:
                res_x_in(o).wait_recv()

        @pl.loop(0, NQ)
        def _(q):
            @pl.when((q == s) & (s > 0))
            def _():
                w_share(q)
                w_ready(q)

            @pl.when(q <= s)
            def _():
                reduce_step(q, jnp.where(s > 2 * q, s, jnp.maximum(2 * (s - q) - 1, 0)))

        @pl.loop(1, NQ)
        def _(q):
            @pl.when((q < s) & (s <= 2 * q))
            def _():
                reduce_step(q, 2 * (s - q))

        @pl.when(s < NQ - 2)
        def _():
            w_pass(s + 2)

        @pl.when(s < NZ - 2)
        def _():
            h_pass(s + 2)

        @pl.when(s < NZ - 3)
        def _():
            h_send(s + 3)

        @pl.when(s == 3)
        def _():
            for o in others:
                q_x(o).start()

        @pl.when(s == 4)
        def _():
            for o in others:
                res_x(o).start()
            wq_local().wait()
            for o in (1, 3, 2):
                q_x_in(o).wait_recv()
            for side in range(2):
                q_y(side).start()

        @pl.when(s == 5)
        def _():
            for side in range(2):
                q_y_in(side).wait_recv()
                q_forward(side).start()

        @pl.when(s == 6)
        def _():
            for side in range(2):
                q_forward_in(side).wait_recv()
            q_c().start()

    q_c_in().wait_recv()
    for i in range(2 * NY):
        packed = [wqp[o, i, 256:384] for o in range(NX)]
        for j in range(2):
            kvw[i * 256 + j * 128 : i * 256 + (j + 1) * 128] = jnp.concatenate(
                [p[:, j * 64 : (j + 1) * 64] for p in packed], axis=1
            )

    @pl.loop(0, NZ)
    def _(k):
        @pl.when(k > 0)
        def _():
            @pl.loop(0, NQ)
            def _(q):
                gather_step(q, k)

        project_step(k)

        @pl.when(k >= 2)
        def _():
            combine_step(k - 2)

    @pl.loop(NZ - 2, NZ)
    def _(k):
        combine_step(k)

    @pl.loop(0, NQ)
    def _(q):
        nr_local(q).wait()
        for o in (1, 2, 3):
            nr_x_in(q, o).wait_recv()
            nr_x(q, o).wait_send()
            w_x(q, o).wait_send()
        for side in range(2):
            w_y(q, side).wait_send()
            w_forward(q, side).wait_send()
        w_c(q).wait_send()

    for o in (1, 2, 3):
        q_x(o).wait_send()
        res_x(o).wait_send()
    for side in range(2):
        q_y(side).wait_send()
        q_forward(side).wait_send()
    q_c().wait_send()

    @pl.loop(0, NZ)
    def _(k):
        for side in range(2):
            h_direct(k, side).wait_send()
            h_forward(k, side).wait_send()
        for o in (1, 2, 3):
            part_x(k, o).wait_send()

    @pl.loop(0, NZ - 1)
    def _(k):
        for q in range(NQ):
            for side in range(2):
                ring(rsb, rs_s, rs_r, q, k, side).wait_send()
                ring(yb, ag_s, ag_r, q, k, side).wait_send()


def per_device(
    hidden,
    residual,
    down_weight,
    norm_gain,
    query_codes,
    query_scales,
    pair_codes,
    pair_scales,
    input_groups,
    query_bias,
    pair_bias,
):
    depth = hidden.shape[1]
    dma = pltpu.SemaphoreType.DMA
    pairs = []
    for shape in (
        (8, 4), (NQ, 3), (NQ, 4), (NQ,), (3,), (4,), (1,),
        (3,), (NQ, 7, 2), (NQ, 7, 2), (NQ, 3), (8, 3),
    ):
        pairs += [dma(shape), dma(shape)]
    new_residual, queries, key_values = pl.pallas_call(
        kernel,
        out_shape=(
            pltpu.VMEM(residual.shape, BF16),
            pltpu.VMEM((4, 8, 32, 128), BF16),
            pltpu.VMEM((2, 4, 8, 32, 32), BF16),
        ),
        in_specs=[pl.BlockSpec(memory_space=pl.ANY)] * 5 + [pl.BlockSpec(memory_space=pltpu.VMEM)] * 6,
        out_specs=(
            pl.BlockSpec(memory_space=pltpu.VMEM),
            pl.BlockSpec(memory_space=pltpu.VMEM),
            pl.BlockSpec(memory_space=pltpu.VMEM),
        ),
        scratch_shapes=[
            pltpu.VMEM((NQ, NX, 4, depth, 128), BF16),
            pltpu.VMEM((NX, NZ, 4, 32, depth), BF16),
            pltpu.VMEM((NQ, NZ, 4, 32, QW), BF16),
            pltpu.VMEM((NQ, NZ, 4, 32, QW), BF16),
            pltpu.VMEM((NX, 384, 128), BF16),
            pltpu.VMEM((NX, 256, 128), BF16),
            pltpu.VMEM((NX, 2, 32, 256), BF16),
            pltpu.VMEM((NX, 8, 384, 128), BF16),
            pltpu.VMEM((XW, 256), BF16),
            pltpu.VMEM((3, NZ, 128, 256), BF16),
            pltpu.VMEM((NZ, NX, 128, 256), BF16),
            pltpu.VMEM((4, 32, XW), BF16),
            pltpu.VMEM((NX * XW // 128, 128), F32),
            pltpu.VMEM((depth, 1024), BF16),
            dma((1,)), dma((NQ, 4)), dma((1,)), dma((1,)), dma((NQ,)), dma((NX, 2)),
        ] + pairs,
        compiler_params=pltpu.CompilerParams(
            collective_id=0, has_side_effects=True, vmem_limit_bytes=58 * 2**20
        ),
        cost_estimate=pl.CostEstimate(flops=12_000_000_000, bytes_accessed=14_000_000, transcendentals=0),
    )(
        hidden.T,
        residual,
        down_weight,
        query_codes,
        jnp.transpose(pair_codes, (0, 2, 1)),
        input_groups.reshape(-1, 128),
        norm_gain.reshape(-1, 128),
        query_scales,
        jnp.transpose(pair_scales, (0, 2, 1)),
        query_bias.reshape(1, 128),
        pair_bias,
    )
    return new_residual, queries.reshape(1024, 128), key_values.reshape(2, 1024, 32)


def solution(mesh):
    in_specs = (
        P("dp", "tensor"),
        P(("dp", "tensor"), None),
        P("tensor", None),
        P(),
        P(None, "tensor"),
        P(None, "tensor"),
        P(None, None, "tensor"),
        P(None, None, "tensor"),
        P(),
        P("tensor"),
        P(None, "tensor"),
    )
    out_specs = (P(("dp", "tensor"), None), P("dp", "tensor"), P(None, "dp", "tensor"))
    return jax.shard_map(
        per_device, mesh=mesh, in_specs=in_specs, out_specs=out_specs, check_vma=False
    )
```

```python
import jax
import jax.numpy as jnp
from jax import lax
from jax.experimental import pallas as pl
from jax.experimental.pallas import tpu as pltpu
from jax.sharding import PartitionSpec as P

MESH = pl.DeviceIdType.MESH
NX, NZ, NY, NC = 4, 8, 4, 2
F32, BF16 = jnp.float32, jnp.bfloat16
NQ, QW = 4, 512
XW = NQ * QW


def kernel(
    hid, res, w, qcodes, pcodes, groups, gains, qscales, pscales, qbias, pbias, nr_out, q_out, kv_out,
    wb, hb, rsb, yb, wq, qc, pc, wqp, kvw, part, snd, resb, gainf, ht,
    l_h, l_w, l_r, l_q, l_n, l_c,
    h_s, h_r, w_s, w_r, wy_s, wy_r, wc_s, wc_r, q_s, q_r, qy_s, qy_r, qc_s, qc_r,
    r_s, r_r, rs_s, rs_r, ag_s, ag_r, n_s, n_r, p_s, p_r,
):
    t, d = lax.axis_index("tensor"), lax.axis_index("dp")
    x, z = t // NZ, t % NZ
    y, c = d // NC, d % NC
    depth = hid.shape[0]
    half = depth // 2
    cut = half // 32 * 16 + 16

    def at(xx, zz, yy, cc):
        return {"tensor": xx * NZ + zz, "dp": yy * NC + cc}

    x_place = [(x + o) % NX for o in range(NX)]
    y_place = [(y + o) % NY for o in range(NY)]
    x_device = [at(p, z, y, c) for p in x_place]
    y_device = [at(x, z, p, c) for p in y_place]
    z_device = {o: at(x, (z + o + NZ) % NZ, y, c) for o in (1, -1)}

    def to_x(o):
        return x_device[o % NX]

    def to_z(o):
        return z_device[o]

    def to_y(o):
        return y_device[o % NY]

    sibling = at(x, z, y, 1 - c)

    def remote(src, dst, ss, rs, device):
        return pltpu.make_async_remote_copy(
            src_ref=src, dst_ref=dst, send_sem=ss, recv_sem=rs, device_id=device, device_id_type=MESH
        )

    def xs(o):
        return x_place[o % NX]

    def ys(o):
        return y_place[o % NY]

    step_of = (1, 3)

    def hid_local():
        return pltpu.make_async_copy(hid, ht, l_h.at[0])

    def w_local(q, i):
        return pltpu.make_async_copy(
            w.at[:, pl.ds(x * XW + q * QW + i * 128, 128)], wb.at[q, 0, i], l_w.at[q, i]
        )

    def res_local():
        return pltpu.make_async_copy(res.at[:, pl.ds(x * XW, XW)], resb.at[x], l_r.at[0])

    rank = c * NY + y

    def wq_local():
        return pltpu.make_async_copy(wq.at[x], wqp.at[0, rank], l_q.at[0])

    def codes_local(o):
        rows = pl.ds(pl.multiple_of(o * XW + rank * 256, 256), 256)
        return (
            pltpu.make_async_copy(qcodes.at[rows], qc.at[o], l_c.at[o, 0]),
            pltpu.make_async_copy(pcodes.at[:, :, rows], pc.at[o], l_c.at[o, 1]),
        )

    def nr_local(q):
        return pltpu.make_async_copy(
            yb.at[q, 0, x], nr_out.at[:, pl.ds(x * XW + q * QW, QW)], l_n.at[q]
        )

    def h_direct(u, side):
        return remote(
            hb.at[0, u], hb.at[NX - step_of[side], u], h_s.at[u, side], h_r.at[u, side], to_x(step_of[side])
        )

    def h_direct_in(u, side):
        ref = hb.at[NX - step_of[side], u]
        return remote(ref, ref, h_s.at[u, side], h_r.at[u, side], to_x(step_of[side]))

    def h_forward(u, side):
        rows = pl.ds(2 * side, 2)
        return remote(
            hb.at[NX - step_of[side], u, rows], hb.at[2, u, rows],
            h_s.at[u, 2 + side], h_r.at[u, 2 + side], to_x(step_of[side]),
        )

    def h_forward_in(u, side):
        ref = hb.at[2, u, pl.ds(2 * side, 2)]
        return remote(ref, ref, h_s.at[u, 2 + side], h_r.at[u, 2 + side], to_x(step_of[side]))

    def w_x(q, o):
        cols = pl.ds(xs(o) * XW + q * QW + y * 128, 128)
        rows = pl.ds(c * half, half)
        return remote(
            w.at[rows, cols], wb.at[q, NX - o, y, rows], w_s.at[q, o - 1], w_r.at[q, o - 1], to_x(o)
        )

    def w_x_in(q, o):
        ref = wb.at[q, NX - o, y, pl.ds(c * half, half)]
        return remote(ref, ref, w_s.at[q, o - 1], w_r.at[q, o - 1], to_x(o))

    def w_y(q, side):
        ref = wb.at[q, pl.ds(1, NX - 1), y, pl.ds(c * half, half)]
        return remote(ref, ref, wy_s.at[q, side], wy_r.at[q, side], to_y(step_of[side]))

    def w_y_in(q, side):
        ref = wb.at[q, pl.ds(1, NX - 1), ys(NY - step_of[side]), pl.ds(c * half, half)]
        return remote(ref, ref, wy_s.at[q, side], wy_r.at[q, side], to_y(step_of[side]))

    def w_part(q, yy, side):
        rows = pl.ds(c * half, cut) if side == 0 else pl.ds(c * half + cut, half - cut)
        return wb.at[q, pl.ds(1, NX - 1), yy, rows]

    def w_forward(q, side):
        ref = w_part(q, ys(NY - step_of[side]), side)
        return remote(ref, ref, wy_s.at[q, 2 + side], wy_r.at[q, 2 + side], to_y(step_of[side]))

    def w_forward_in(q, side):
        ref = w_part(q, ys(2), side)
        return remote(ref, ref, wy_s.at[q, 2 + side], wy_r.at[q, 2 + side], to_y(step_of[side]))

    def w_c(q):
        ref = wb.at[q, pl.ds(1, NX - 1), :, pl.ds(c * half, half)]
        return remote(ref, ref, wc_s.at[q], wc_r.at[q], sibling)

    def w_c_in(q):
        ref = wb.at[q, pl.ds(1, NX - 1), :, pl.ds((1 - c) * half, half)]
        return remote(ref, ref, wc_s.at[q], wc_r.at[q], sibling)

    def q_x(o):
        return remote(wq.at[xs(o)], wqp.at[NX - o, rank], q_s.at[o - 1], q_r.at[o - 1], to_x(o))

    def q_x_in(o):
        ref = wqp.at[NX - o, rank]
        return remote(ref, ref, q_s.at[o - 1], q_r.at[o - 1], to_x(o))

    def q_y(side):
        ref = wqp.at[:, rank]
        return remote(ref, ref, qy_s.at[side], qy_r.at[side], to_y(step_of[side]))

    def q_y_in(side):
        ref = wqp.at[:, c * NY + ys(NY - step_of[side])]
        return remote(ref, ref, qy_s.at[side], qy_r.at[side], to_y(step_of[side]))

    def q_forward(side):
        ref = wqp.at[:, c * NY + ys(NY - step_of[side]), pl.ds(192 * side, 192)]
        return remote(ref, ref, qy_s.at[2 + side], qy_r.at[2 + side], to_y(step_of[side]))

    def q_forward_in(side):
        ref = wqp.at[:, c * NY + ys(2), pl.ds(192 * side, 192)]
        return remote(ref, ref, qy_s.at[2 + side], qy_r.at[2 + side], to_y(step_of[side]))

    def q_c():
        ref = wqp.at[:, pl.ds(c * NY, NY)]
        return remote(ref, ref, qc_s.at[0], qc_r.at[0], sibling)

    def q_c_in():
        ref = wqp.at[:, pl.ds((1 - c) * NY, NY)]
        return remote(ref, ref, qc_s.at[0], qc_r.at[0], sibling)

    def res_x(o):
        return remote(
            res.at[:, pl.ds(xs(o) * XW, XW)], resb.at[x], r_s.at[o - 1], r_r.at[o - 1], to_x(o)
        )

    def res_x_in(o):
        ref = resb.at[xs(NX - o)]
        return remote(ref, ref, r_s.at[o - 1], r_r.at[o - 1], to_x(o))

    def ring(buf, ss, rs, q, k, side):
        rows = pl.ds(2 * side, 2)
        return remote(
            buf.at[q, k, rows], buf.at[q, k + 1, rows],
            ss.at[q, k, side], rs.at[q, k, side], to_z(1 if side == 0 else -1),
        )

    def ring_in(buf, ss, rs, q, k, side):
        ref = buf.at[q, k, pl.ds(2 * side, 2)]
        return remote(ref, ref, ss.at[q, k - 1, side], rs.at[q, k - 1, side], to_z(1))

    def nr_x(q, o):
        return remote(
            yb.at[q, 0, xs(o)], nr_out.at[:, pl.ds(x * XW + q * QW, QW)],
            n_s.at[q, o - 1], n_r.at[q, o - 1], to_x(o),
        )

    def nr_x_in(q, o):
        ref = nr_out.at[:, pl.ds(xs(NX - o) * XW + q * QW, QW)]
        return remote(ref, ref, n_s.at[q, o - 1], n_r.at[q, o - 1], to_x(o))

    def part_x(k, o):
        return remote(snd.at[k, o], part.at[o - 1, k], p_s.at[k, o - 1], p_r.at[k, o - 1], to_x(o))

    others = (2, 1, 3)

    def h_send(u):
        for side in range(2):
            h_direct(u, side).start()

    def turn_hidden():
        hid_local().wait()
        for b in range(8):
            turned = ht[:, b * 128 : (b + 1) * 128].astype(F32).T.astype(BF16)
            turned = jnp.concatenate([turned, jnp.zeros((128, hb.shape[-1] - depth), BF16)], axis=1)
            for i in range(4):
                xt, zc = b // 2, (b % 2) * 4 + i
                u = (z + 2 * NZ - 1 - zc) % NZ if xt < 2 else (zc + 2 * NZ - 1 - z) % NZ
                hb[0, u, xt] = turned[i * 32 : (i + 1) * 32]

    def h_pass(u):
        for side in range(2):
            h_direct_in(u, side).wait_recv()
            h_forward(u, side).start()

    def h_ready(u):
        for side in range(2):
            h_forward_in(u, side).wait_recv()

    def w_send(q):
        for o in others:
            w_x(q, o).start()

    def w_spread(q):
        for o in (1, 3, 2):
            w_x_in(q, o).wait_recv()
        for side in range(2):
            w_y(q, side).start()

    def w_pass(q):
        for side in range(2):
            w_y_in(q, side).wait_recv()
            w_forward(q, side).start()

    def w_share(q):
        for side in range(2):
            w_forward_in(q, side).wait_recv()
        w_c(q).start()

    def w_ready(q):
        for i in range(4):
            w_local(q, i).wait()
        w_c_in(q).wait_recv()

    def scale_weights():
        row = lax.broadcasted_iota(jnp.int32, (qscales.shape[0], 128), 0)
        gainf[...] = gains[...].astype(F32)
        for o in range(NX):
            for copy in codes_local(o):
                copy.wait()
            picked = []
            for j in range(2):
                line = pl.ds(o * (XW // 128) + rank * 2 + j, 1)
                picked.append(jnp.where(row == groups[line, :], gainf[line, :], 0.0).astype(BF16))
            picked = jnp.concatenate(picked, axis=1)
            factor = lax.dot_general(
                picked, qscales[...], (((0,), (0,)), ((), ())), preferred_element_type=F32
            )
            wq[o, 0:256] = (qc[o].astype(F32) * factor).astype(BF16)
            factor = jnp.dot(pscales[...].reshape(64, -1), picked, preferred_element_type=F32)
            flat = pc[o].reshape(64, 256).astype(F32) * factor
            packed = jnp.concatenate([flat[:, :128], flat[:, 128:]], axis=0)
            wq[o, 256:384] = packed.T.astype(BF16)
        wq_local().start()

    def reduce_step(q, k):
        acc = jnp.zeros((128, QW), F32)
        for o in range(NX):
            weight = jnp.concatenate([wb[q, o, i] for i in range(4)], axis=1)
            acc += jnp.dot(hb[o, k].reshape(128, hb.shape[-1])[:, :depth], weight, preferred_element_type=F32)

        @pl.when(k > 0)
        def _():
            for side in range(2):
                ring_in(rsb, rs_s, rs_r, q, k, side).wait_recv()

        acc += rsb[q, k].reshape(128, QW).astype(F32)

        @pl.when(k < NZ - 1)
        def _():
            rsb[q, k] = acc.astype(BF16).reshape(4, 32, QW)
            for side in range(2):
                ring(rsb, rs_s, rs_r, q, k, side).start()

        @pl.when(k == NZ - 1)
        def _():
            own = resb[:, :, pl.ds(pl.multiple_of(q * QW, QW), QW)].reshape(128, QW).astype(F32)
            yb[q, 0] = (acc + own).astype(BF16).reshape(4, 32, QW)
            for side in range(2):
                ring(yb, ag_s, ag_r, q, 0, side).start()
            nr_local(q).start()
            for o in others:
                nr_x(q, o).start()

    def gather_step(q, k):
        for side in range(2):
            ring_in(yb, ag_s, ag_r, q, k, side).wait_recv()

        @pl.when(k < NZ - 1)
        def _():
            for side in range(2):
                ring(yb, ag_s, ag_r, q, k, side).start()

    def project_step(k):
        acc_q = [jnp.zeros((128, 256), F32), jnp.zeros((128, 256), F32)]
        acc_kv = jnp.zeros((128, 256), F32)
        squares = jnp.zeros((128, 1), F32)
        for q in range(NQ):
            rows = yb[q, k].reshape(128, QW)
            for pair in range(2):
                weight = jnp.concatenate(
                    [
                        jnp.concatenate([wqp[2 * pair + i, 2 * q + j, 0:256] for j in range(2)], axis=0)
                        for i in range(2)
                    ],
                    axis=1,
                )
                acc_q[pair] += jnp.dot(rows, weight, preferred_element_type=F32)
            acc_kv += jnp.dot(rows, kvw[q * QW : (q + 1) * QW], preferred_element_type=F32)
            wide = rows.astype(F32)
            squares += jnp.sum(wide * wide, axis=1, keepdims=True)
        high = squares.astype(BF16).astype(F32)
        low = squares - high
        lane = lax.broadcasted_iota(jnp.int32, (128, 64), 1)
        extra = jnp.where(lane == 0, high, jnp.where(lane == 1, low, 0.0))
        for o in range(NX):
            snd[k, o, :, 0:128] = acc_q[o // 2][:, (o % 2) * 128 : (o % 2 + 1) * 128].astype(BF16)
            snd[k, o, :, 128:256] = jnp.concatenate(
                [acc_kv[:, o * 64 : (o + 1) * 64], extra], axis=1
            ).astype(BF16)
        for o in others:
            part_x(k, o).start()

    def combine_step(k):
        total = snd[k, 0].astype(F32)
        for o in (1, 2, 3):
            part_x(k, o).wait_recv()
            total += part[o - 1, k].astype(F32)
        lane = lax.broadcasted_iota(jnp.int32, (128, 256), 1)
        squares = jnp.sum(jnp.where((lane == 192) | (lane == 193), total, 0.0), axis=1, keepdims=True)
        out = total * lax.rsqrt(squares / (NX * XW) + 1e-6)
        wide_q = (out[:, :128] + qbias[...].astype(F32)).astype(BF16)
        wide_k = (out[:, 128:160] + pbias[0:1, :].astype(F32)).astype(BF16)
        wide_v = (out[:, 160:192] + pbias[1:2, :].astype(F32)).astype(BF16)
        for side in range(2):
            zz = (z + NZ - k) % NZ if side == 0 else (z + k) % NZ
            for i in range(2):
                xt = 2 * side + i
                rows = slice(xt * 32, (xt + 1) * 32)
                q_out[xt, zz] = wide_q[rows]
                kv_out[0, xt, zz] = wide_k[rows]
                kv_out[1, xt, zz] = wide_v[rows]

    barrier = pltpu.get_barrier_semaphore()
    friends = [to_x(1), to_x(2), to_x(3), to_z(1), to_z(-1), to_y(1), to_y(3), sibling]
    for friend in friends:
        pl.semaphore_signal(barrier, inc=1, device_id=friend, device_id_type=MESH)
    hid_local().start()
    for q in range(NQ):
        for i in range(4):
            w_local(q, i).start()
    res_local().start()
    for o in range(NX):
        for copy in codes_local(o):
            copy.start()
    for q in range(NQ):
        rsb[q, 0] = jnp.zeros(rsb.shape[2:], BF16)

    pl.semaphore_wait(barrier, len(friends))

    w_send(0)
    turn_hidden()
    h_send(0)
    w_spread(0)
    w_send(1)
    w_send(2)
    h_pass(0)
    h_send(1)
    w_pass(0)
    w_spread(1)
    w_send(3)
    w_spread(2)
    w_share(0)
    h_pass(1)
    h_send(2)
    w_ready(0)
    w_pass(1)
    w_spread(3)

    @pl.loop(0, NZ)
    def _(s):
        h_ready(s)

        @pl.when(s == NZ - 1)
        def _():
            res_local().wait()
            for o in others:
                res_x_in(o).wait_recv()

        @pl.loop(0, NQ)
        def _(q):
            @pl.when((q == s) & (s > 0))
            def _():
                w_share(q)
                w_ready(q)

            @pl.when(q <= s)
            def _():
                reduce_step(q, jnp.where(s > 2 * q, s, jnp.maximum(2 * (s - q) - 1, 0)))

        @pl.loop(1, NQ)
        def _(q):
            @pl.when((q < s) & (s <= 2 * q))
            def _():
                reduce_step(q, 2 * (s - q))

        @pl.when(s < NQ - 2)
        def _():
            w_pass(s + 2)

        @pl.when(s < NZ - 2)
        def _():
            h_pass(s + 2)

        @pl.when(s < NZ - 3)
        def _():
            h_send(s + 3)

        @pl.when(s == 3)
        def _():
            scale_weights()
            for o in others:
                q_x(o).start()

        @pl.when(s == 4)
        def _():
            for o in others:
                res_x(o).start()
            wq_local().wait()
            for o in (1, 3, 2):
                q_x_in(o).wait_recv()
            for side in range(2):
                q_y(side).start()

        @pl.when(s == 5)
        def _():
            for side in range(2):
                q_y_in(side).wait_recv()
                q_forward(side).start()

        @pl.when(s == 6)
        def _():
            for side in range(2):
                q_forward_in(side).wait_recv()
            q_c().start()

    def finish_quarter(q):
        nr_local(q).wait()
        for o in (1, 2, 3):
            nr_x_in(q, o).wait_recv()
            nr_x(q, o).wait_send()
            w_x(q, o).wait_send()
        for side in range(2):
            w_y(q, side).wait_send()
            w_forward(q, side).wait_send()
        w_c(q).wait_send()

    def finish_step(k):
        for side in range(2):
            h_direct(k, side).wait_send()
            h_forward(k, side).wait_send()

        @pl.loop(0, NQ)
        def _(q):
            for side in range(2):
                ring(rsb, rs_s, rs_r, q, k, side).wait_send()
                ring(yb, ag_s, ag_r, q, k, side).wait_send()

    def finish_part(k):
        for o in (1, 2, 3):
            part_x(k, o).wait_send()

    q_c_in().wait_recv()
    for i in range(2 * NY):
        packed = [wqp[o, i, 256:384] for o in range(NX)]
        for j in range(2):
            kvw[i * 256 + j * 128 : i * 256 + (j + 1) * 128] = jnp.concatenate(
                [p[:, j * 64 : (j + 1) * 64] for p in packed], axis=1
            )

    @pl.loop(0, NZ)
    def _(k):
        @pl.when(k > 0)
        def _():
            @pl.loop(0, NQ)
            def _(q):
                gather_step(q, k)

        project_step(k)

        @pl.when(k >= 2)
        def _():
            combine_step(k - 2)
            finish_part(k - 2)

        @pl.when(k > 0)
        def _():
            finish_step(k - 1)

        @pl.when((k > 1) & (k < NQ + 2))
        def _():
            finish_quarter(k - 2)

        @pl.when(k == 1)
        def _():
            for o in (1, 2, 3):
                q_x(o).wait_send()
                res_x(o).wait_send()
            for side in range(2):
                q_y(side).wait_send()
                q_forward(side).wait_send()
                h_direct(NZ - 1, side).wait_send()
                h_forward(NZ - 1, side).wait_send()
            q_c().wait_send()

    @pl.loop(NZ - 2, NZ)
    def _(k):
        combine_step(k)
        finish_part(k)


def per_device(
    hidden,
    residual,
    down_weight,
    norm_gain,
    query_codes,
    query_scales,
    pair_codes,
    pair_scales,
    input_groups,
    query_bias,
    pair_bias,
):
    depth = hidden.shape[1]
    wide_depth = (depth + 127) // 128 * 128
    dma = pltpu.SemaphoreType.DMA
    pairs = []
    for shape in (
        (8, 4), (NQ, 3), (NQ, 4), (NQ,), (3,), (4,), (1,),
        (3,), (NQ, 7, 2), (NQ, 7, 2), (NQ, 3), (8, 3),
    ):
        pairs += [dma(shape), dma(shape)]
    new_residual, queries, key_values = pl.pallas_call(
        kernel,
        out_shape=(
            pltpu.VMEM(residual.shape, BF16),
            pltpu.VMEM((4, 8, 32, 128), BF16),
            pltpu.VMEM((2, 4, 8, 32, 32), BF16),
        ),
        in_specs=[pl.BlockSpec(memory_space=pl.ANY)] * 5 + [pl.BlockSpec(memory_space=pltpu.VMEM)] * 6,
        out_specs=(
            pl.BlockSpec(memory_space=pltpu.VMEM),
            pl.BlockSpec(memory_space=pltpu.VMEM),
            pl.BlockSpec(memory_space=pltpu.VMEM),
        ),
        scratch_shapes=[
            pltpu.VMEM((NQ, NX, 4, depth, 128), BF16),
            pltpu.VMEM((NX, NZ, 4, 32, wide_depth), BF16),
            pltpu.VMEM((NQ, NZ, 4, 32, QW), BF16),
            pltpu.VMEM((NQ, NZ, 4, 32, QW), BF16),
            pltpu.VMEM((NX, 384, 128), BF16),
            pltpu.VMEM((NX, 256, 128), BF16),
            pltpu.VMEM((NX, 2, 32, 256), BF16),
            pltpu.VMEM((NX, 8, 384, 128), BF16),
            pltpu.VMEM((XW, 256), BF16),
            pltpu.VMEM((3, NZ, 128, 256), BF16),
            pltpu.VMEM((NZ, NX, 128, 256), BF16),
            pltpu.VMEM((4, 32, XW), BF16),
            pltpu.VMEM((NX * XW // 128, 128), F32),
            pltpu.VMEM((depth, 1024), BF16),
            dma((1,)), dma((NQ, 4)), dma((1,)), dma((1,)), dma((NQ,)), dma((NX, 2)),
        ] + pairs,
        compiler_params=pltpu.CompilerParams(
            collective_id=0, has_side_effects=True, vmem_limit_bytes=58 * 2**20
        ),
        cost_estimate=pl.CostEstimate(flops=12_000_000_000, bytes_accessed=14_000_000, transcendentals=0),
    )(
        hidden.T,
        residual,
        down_weight,
        query_codes,
        jnp.transpose(pair_codes, (0, 2, 1)),
        input_groups.reshape(-1, 128),
        norm_gain.reshape(-1, 128),
        query_scales,
        jnp.transpose(pair_scales, (0, 2, 1)),
        query_bias.reshape(1, 128),
        pair_bias,
    )
    return new_residual, queries.reshape(1024, 128), key_values.reshape(2, 1024, 32)


def solution(mesh):
    in_specs = (
        P("dp", "tensor"),
        P(("dp", "tensor"), None),
        P("tensor", None),
        P(),
        P(None, "tensor"),
        P(None, "tensor"),
        P(None, None, "tensor"),
        P(None, None, "tensor"),
        P(),
        P("tensor"),
        P(None, "tensor"),
    )
    out_specs = (P(("dp", "tensor"), None), P("dp", "tensor"), P(None, "dp", "tensor"))
    return jax.shard_map(
        per_device, mesh=mesh, in_specs=in_specs, out_specs=out_specs, check_vma=False
    )
```

```python
import jax
import jax.numpy as jnp
from jax import lax
from jax.experimental import pallas as pl
from jax.experimental.pallas import tpu as pltpu
from jax.sharding import PartitionSpec as P

MESH = pl.DeviceIdType.MESH
NX, NZ, NY, NC = 4, 8, 4, 2
F32, BF16 = jnp.float32, jnp.bfloat16
NQ, QW = 4, 512
XW = NQ * QW


def kernel(
    hid, res, w, qcodes, pcodes, groups, gains, qscales, pscales, qbias, pbias, nr_out, q_out, kv_out,
    wb, hb, rsb, yb, wq, qc, pc, wqp, kvw, part, snd, resb, gainf, ht,
    l_h, l_w, l_r, l_q, l_n, l_c,
    h_s, h_r, w_s, w_r, wy_s, wy_r, wc_s, wc_r, q_s, q_r, qy_s, qy_r, qc_s, qc_r,
    r_s, r_r, rs_s, rs_r, ag_s, ag_r, n_s, n_r, p_s, p_r,
):
    t, d = lax.axis_index("tensor"), lax.axis_index("dp")
    x, z = t // NZ, t % NZ
    y, c = d // NC, d % NC
    depth = hid.shape[0]
    half = depth // 2
    cut = half // 32 * 16 + 16

    def at(xx, zz, yy, cc):
        return {"tensor": xx * NZ + zz, "dp": yy * NC + cc}

    x_place = [(x + o) % NX for o in range(NX)]
    y_place = [(y + o) % NY for o in range(NY)]
    x_device = [at(p, z, y, c) for p in x_place]
    y_device = [at(x, z, p, c) for p in y_place]
    z_device = {o: at(x, (z + o + NZ) % NZ, y, c) for o in (1, -1)}

    def to_x(o):
        return x_device[o % NX]

    def to_z(o):
        return z_device[o]

    def to_y(o):
        return y_device[o % NY]

    sibling = at(x, z, y, 1 - c)

    def remote(src, dst, ss, rs, device):
        return pltpu.make_async_remote_copy(
            src_ref=src, dst_ref=dst, send_sem=ss, recv_sem=rs, device_id=device, device_id_type=MESH
        )

    def xs(o):
        return x_place[o % NX]

    def ys(o):
        return y_place[o % NY]

    step_of = (1, 3)

    def hid_local():
        return pltpu.make_async_copy(hid, ht, l_h.at[0])

    def w_local(q, i):
        return pltpu.make_async_copy(
            w.at[:, pl.ds(x * XW + q * QW + i * 128, 128)], wb.at[q, 0, i], l_w.at[q, i]
        )

    def res_local():
        return pltpu.make_async_copy(res.at[:, pl.ds(x * XW, XW)], resb.at[x], l_r.at[0])

    rank = c * NY + y

    def wq_local():
        return pltpu.make_async_copy(wq.at[x], wqp.at[0, rank], l_q.at[0])

    def codes_local(o):
        rows = pl.ds(pl.multiple_of(o * XW + rank * 256, 256), 256)
        return (
            pltpu.make_async_copy(qcodes.at[rows], qc.at[o], l_c.at[o, 0]),
            pltpu.make_async_copy(pcodes.at[:, :, rows], pc.at[o], l_c.at[o, 1]),
        )

    def nr_local(q):
        return pltpu.make_async_copy(
            yb.at[q, 0, x], nr_out.at[:, pl.ds(x * XW + q * QW, QW)], l_n.at[q]
        )

    def h_direct(u, side):
        return remote(
            hb.at[0, u], hb.at[NX - step_of[side], u], h_s.at[u, side], h_r.at[u, side], to_x(step_of[side])
        )

    def h_direct_in(u, side):
        ref = hb.at[NX - step_of[side], u]
        return remote(ref, ref, h_s.at[u, side], h_r.at[u, side], to_x(step_of[side]))

    def h_forward(u, side):
        rows = pl.ds(2 * side, 2)
        return remote(
            hb.at[NX - step_of[side], u, rows], hb.at[2, u, rows],
            h_s.at[u, 2 + side], h_r.at[u, 2 + side], to_x(step_of[side]),
        )

    def h_forward_in(u, side):
        ref = hb.at[2, u, pl.ds(2 * side, 2)]
        return remote(ref, ref, h_s.at[u, 2 + side], h_r.at[u, 2 + side], to_x(step_of[side]))

    def w_x(q, o):
        cols = pl.ds(xs(o) * XW + q * QW + y * 128, 128)
        rows = pl.ds(c * half, half)
        return remote(
            w.at[rows, cols], wb.at[q, NX - o, y, rows], w_s.at[q, o - 1], w_r.at[q, o - 1], to_x(o)
        )

    def w_x_in(q, o):
        ref = wb.at[q, NX - o, y, pl.ds(c * half, half)]
        return remote(ref, ref, w_s.at[q, o - 1], w_r.at[q, o - 1], to_x(o))

    def w_y(q, side):
        ref = wb.at[q, pl.ds(1, NX - 1), y, pl.ds(c * half, half)]
        return remote(ref, ref, wy_s.at[q, side], wy_r.at[q, side], to_y(step_of[side]))

    def w_y_in(q, side):
        ref = wb.at[q, pl.ds(1, NX - 1), ys(NY - step_of[side]), pl.ds(c * half, half)]
        return remote(ref, ref, wy_s.at[q, side], wy_r.at[q, side], to_y(step_of[side]))

    def w_part(q, yy, side):
        rows = pl.ds(c * half, cut) if side == 0 else pl.ds(c * half + cut, half - cut)
        return wb.at[q, pl.ds(1, NX - 1), yy, rows]

    def w_forward(q, side):
        ref = w_part(q, ys(NY - step_of[side]), side)
        return remote(ref, ref, wy_s.at[q, 2 + side], wy_r.at[q, 2 + side], to_y(step_of[side]))

    def w_forward_in(q, side):
        ref = w_part(q, ys(2), side)
        return remote(ref, ref, wy_s.at[q, 2 + side], wy_r.at[q, 2 + side], to_y(step_of[side]))

    def w_c(q):
        ref = wb.at[q, pl.ds(1, NX - 1), :, pl.ds(c * half, half)]
        return remote(ref, ref, wc_s.at[q], wc_r.at[q], sibling)

    def w_c_in(q):
        ref = wb.at[q, pl.ds(1, NX - 1), :, pl.ds((1 - c) * half, half)]
        return remote(ref, ref, wc_s.at[q], wc_r.at[q], sibling)

    def q_x(o):
        return remote(wq.at[xs(o)], wqp.at[NX - o, rank], q_s.at[o - 1], q_r.at[o - 1], to_x(o))

    def q_x_in(o):
        ref = wqp.at[NX - o, rank]
        return remote(ref, ref, q_s.at[o - 1], q_r.at[o - 1], to_x(o))

    def q_y(side):
        ref = wqp.at[:, rank]
        return remote(ref, ref, qy_s.at[side], qy_r.at[side], to_y(step_of[side]))

    def q_y_in(side):
        ref = wqp.at[:, c * NY + ys(NY - step_of[side])]
        return remote(ref, ref, qy_s.at[side], qy_r.at[side], to_y(step_of[side]))

    def q_forward(side):
        ref = wqp.at[:, c * NY + ys(NY - step_of[side]), pl.ds(192 * side, 192)]
        return remote(ref, ref, qy_s.at[2 + side], qy_r.at[2 + side], to_y(step_of[side]))

    def q_forward_in(side):
        ref = wqp.at[:, c * NY + ys(2), pl.ds(192 * side, 192)]
        return remote(ref, ref, qy_s.at[2 + side], qy_r.at[2 + side], to_y(step_of[side]))

    def q_c():
        ref = wqp.at[:, pl.ds(c * NY, NY)]
        return remote(ref, ref, qc_s.at[0], qc_r.at[0], sibling)

    def q_c_in():
        ref = wqp.at[:, pl.ds((1 - c) * NY, NY)]
        return remote(ref, ref, qc_s.at[0], qc_r.at[0], sibling)

    def res_x(o):
        return remote(
            res.at[:, pl.ds(xs(o) * XW, XW)], resb.at[x], r_s.at[o - 1], r_r.at[o - 1], to_x(o)
        )

    def res_x_in(o):
        ref = resb.at[xs(NX - o)]
        return remote(ref, ref, r_s.at[o - 1], r_r.at[o - 1], to_x(o))

    def ring(buf, ss, rs, q, k, side):
        rows = pl.ds(2 * side, 2)
        return remote(
            buf.at[q, k, rows], buf.at[q, k + 1, rows],
            ss.at[q, k, side], rs.at[q, k, side], to_z(1 if side == 0 else -1),
        )

    def ring_in(buf, ss, rs, q, k, side):
        ref = buf.at[q, k, pl.ds(2 * side, 2)]
        return remote(ref, ref, ss.at[q, k - 1, side], rs.at[q, k - 1, side], to_z(1))

    def nr_x(q, o):
        return remote(
            yb.at[q, 0, xs(o)], nr_out.at[:, pl.ds(x * XW + q * QW, QW)],
            n_s.at[q, o - 1], n_r.at[q, o - 1], to_x(o),
        )

    def nr_x_in(q, o):
        ref = nr_out.at[:, pl.ds(xs(NX - o) * XW + q * QW, QW)]
        return remote(ref, ref, n_s.at[q, o - 1], n_r.at[q, o - 1], to_x(o))

    def part_x(k, o):
        return remote(snd.at[k, o], part.at[o - 1, k], p_s.at[k, o - 1], p_r.at[k, o - 1], to_x(o))

    others = (2, 1, 3)

    def h_send(u):
        for side in range(2):
            h_direct(u, side).start()

    def turn_hidden():
        hid_local().wait()
        for b in range(8):
            turned = ht[:, b * 128 : (b + 1) * 128].astype(F32).T.astype(BF16)
            turned = jnp.concatenate([turned, jnp.zeros((128, hb.shape[-1] - depth), BF16)], axis=1)
            for i in range(4):
                xt, zc = b // 2, (b % 2) * 4 + i
                u = (z + 2 * NZ - 1 - zc) % NZ if xt < 2 else (zc + 2 * NZ - 1 - z) % NZ
                hb[0, u, xt] = turned[i * 32 : (i + 1) * 32]

    def h_pass(u):
        for side in range(2):
            h_direct_in(u, side).wait_recv()
            h_forward(u, side).start()

    def h_ready(u):
        for side in range(2):
            h_forward_in(u, side).wait_recv()

    def w_send(q):
        for o in others:
            w_x(q, o).start()

    def w_spread(q):
        for o in (1, 3, 2):
            w_x_in(q, o).wait_recv()
        for side in range(2):
            w_y(q, side).start()

    def w_pass(q):
        for side in range(2):
            w_y_in(q, side).wait_recv()
            w_forward(q, side).start()

    def w_share(q):
        for side in range(2):
            w_forward_in(q, side).wait_recv()
        w_c(q).start()

    def w_ready(q):
        for i in range(4):
            w_local(q, i).wait()
        w_c_in(q).wait_recv()

    def scale_weights():
        row = lax.broadcasted_iota(jnp.int32, (qscales.shape[0], 128), 0)
        gainf[...] = gains[...].astype(F32)
        for o in range(NX):
            for copy in codes_local(o):
                copy.wait()
            picked = []
            for j in range(2):
                line = pl.ds(o * (XW // 128) + rank * 2 + j, 1)
                picked.append(jnp.where(row == groups[line, :], gainf[line, :], 0.0).astype(BF16))
            picked = jnp.concatenate(picked, axis=1)
            factor = lax.dot_general(
                picked, qscales[...], (((0,), (0,)), ((), ())), preferred_element_type=F32
            )
            wq[o, 0:256] = (qc[o].astype(F32) * factor).astype(BF16)
            factor = jnp.dot(pscales[...].reshape(64, -1), picked, preferred_element_type=F32)
            flat = pc[o].reshape(64, 256).astype(F32) * factor
            packed = jnp.concatenate([flat[:, :128], flat[:, 128:]], axis=0)
            wq[o, 256:384] = packed.T.astype(BF16)
        wq_local().start()

    def reduce_step(q, k):
        acc = jnp.zeros((128, QW), F32)
        for o in range(NX):
            weight = jnp.concatenate([wb[q, o, i] for i in range(4)], axis=1)
            acc += jnp.dot(hb[o, k].reshape(128, hb.shape[-1])[:, :depth], weight, preferred_element_type=F32)

        @pl.when(k > 0)
        def _():
            for side in range(2):
                ring_in(rsb, rs_s, rs_r, q, k, side).wait_recv()

        acc += rsb[q, k].reshape(128, QW).astype(F32)

        @pl.when(k < NZ - 1)
        def _():
            rsb[q, k] = acc.astype(BF16).reshape(4, 32, QW)
            for side in range(2):
                ring(rsb, rs_s, rs_r, q, k, side).start()

        @pl.when(k == NZ - 1)
        def _():
            own = resb[:, :, pl.ds(pl.multiple_of(q * QW, QW), QW)].reshape(128, QW).astype(F32)
            yb[q, 0] = (acc + own).astype(BF16).reshape(4, 32, QW)
            for side in range(2):
                ring(yb, ag_s, ag_r, q, 0, side).start()
            nr_local(q).start()
            for o in others:
                nr_x(q, o).start()

    def gather_step(q, k):
        for side in range(2):
            ring_in(yb, ag_s, ag_r, q, k, side).wait_recv()

        @pl.when(k < NZ - 1)
        def _():
            for side in range(2):
                ring(yb, ag_s, ag_r, q, k, side).start()

    def project_step(k):
        acc_q = [jnp.zeros((128, 256), F32), jnp.zeros((128, 256), F32)]
        acc_kv = jnp.zeros((128, 256), F32)
        squares = jnp.zeros((128, 1), F32)
        for q in range(NQ):
            rows = yb[q, k].reshape(128, QW)
            for pair in range(2):
                weight = jnp.concatenate(
                    [
                        jnp.concatenate([wqp[2 * pair + i, 2 * q + j, 0:256] for j in range(2)], axis=0)
                        for i in range(2)
                    ],
                    axis=1,
                )
                acc_q[pair] += jnp.dot(rows, weight, preferred_element_type=F32)
            acc_kv += jnp.dot(rows, kvw[q * QW : (q + 1) * QW], preferred_element_type=F32)
            wide = rows.astype(F32)
            squares += jnp.sum(wide * wide, axis=1, keepdims=True)
        high = squares.astype(BF16).astype(F32)
        low = squares - high
        lane = lax.broadcasted_iota(jnp.int32, (128, 64), 1)
        extra = jnp.where(lane == 0, high, jnp.where(lane == 1, low, 0.0))
        for o in range(NX):
            snd[k, o, :, 0:128] = acc_q[o // 2][:, (o % 2) * 128 : (o % 2 + 1) * 128].astype(BF16)
            snd[k, o, :, 128:256] = jnp.concatenate(
                [acc_kv[:, o * 64 : (o + 1) * 64], extra], axis=1
            ).astype(BF16)
        for o in others:
            part_x(k, o).start()

    def combine_step(k):
        total = snd[k, 0].astype(F32)
        for o in (1, 2, 3):
            part_x(k, o).wait_recv()
            total += part[o - 1, k].astype(F32)
        lane = lax.broadcasted_iota(jnp.int32, (128, 256), 1)
        squares = jnp.sum(jnp.where((lane == 192) | (lane == 193), total, 0.0), axis=1, keepdims=True)
        out = total * lax.rsqrt(squares / (NX * XW) + 1e-6)
        wide_q = (out[:, :128] + qbias[...].astype(F32)).astype(BF16)
        wide_k = (out[:, 128:160] + pbias[0:1, :].astype(F32)).astype(BF16)
        wide_v = (out[:, 160:192] + pbias[1:2, :].astype(F32)).astype(BF16)
        for side in range(2):
            zz = (z + NZ - k) % NZ if side == 0 else (z + k) % NZ
            for i in range(2):
                xt = 2 * side + i
                rows = slice(xt * 32, (xt + 1) * 32)
                q_out[xt, zz] = wide_q[rows]
                kv_out[0, xt, zz] = wide_k[rows]
                kv_out[1, xt, zz] = wide_v[rows]

    barrier = pltpu.get_barrier_semaphore()
    friends = [to_x(1), to_x(2), to_x(3), to_z(1), to_z(-1), to_y(1), to_y(3), sibling]
    for friend in friends:
        pl.semaphore_signal(barrier, inc=1, device_id=friend, device_id_type=MESH)
    hid_local().start()
    for q in range(NQ):
        for i in range(4):
            w_local(q, i).start()
    res_local().start()
    for o in range(NX):
        for copy in codes_local(o):
            copy.start()
    for q in range(NQ):
        rsb[q, 0] = jnp.zeros(rsb.shape[2:], BF16)

    pl.semaphore_wait(barrier, len(friends))

    w_send(0)
    turn_hidden()
    h_send(0)
    w_spread(0)
    w_send(1)
    w_send(2)
    h_pass(0)
    h_send(1)
    w_pass(0)
    w_spread(1)
    w_send(3)
    w_spread(2)
    w_share(0)
    h_pass(1)
    h_send(2)
    w_ready(0)
    w_pass(1)
    w_spread(3)

    @pl.loop(0, NZ)
    def _(s):
        h_ready(s)

        @pl.when(s == NZ - 1)
        def _():
            res_local().wait()
            for o in others:
                res_x_in(o).wait_recv()

        @pl.loop(0, NQ)
        def _(q):
            @pl.when((q == s) & (s > 0))
            def _():
                w_share(q)
                w_ready(q)

            @pl.when(q <= s)
            def _():
                reduce_step(q, s - q + jnp.minimum(jnp.maximum(s - 4, 0), q))

        @pl.loop(1, NQ)
        def _(q):
            @pl.when((s >= 4) & (s < q + 4))
            def _():
                reduce_step(q, 2 * s - q - 4 + 1)

        @pl.when(s < NQ - 2)
        def _():
            w_pass(s + 2)

        @pl.when(s < NZ - 2)
        def _():
            h_pass(s + 2)

        @pl.when(s < NZ - 3)
        def _():
            h_send(s + 3)

        @pl.when(s == 3)
        def _():
            scale_weights()
            for o in others:
                q_x(o).start()

        @pl.when(s == 4)
        def _():
            for o in others:
                res_x(o).start()
            wq_local().wait()
            for o in (1, 3, 2):
                q_x_in(o).wait_recv()
            for side in range(2):
                q_y(side).start()

        @pl.when(s == 5)
        def _():
            for side in range(2):
                q_y_in(side).wait_recv()
                q_forward(side).start()

        @pl.when(s == 6)
        def _():
            for side in range(2):
                q_forward_in(side).wait_recv()
            q_c().start()

    def finish_quarter(q):
        nr_local(q).wait()
        for o in (1, 2, 3):
            nr_x_in(q, o).wait_recv()
            nr_x(q, o).wait_send()
            w_x(q, o).wait_send()
        for side in range(2):
            w_y(q, side).wait_send()
            w_forward(q, side).wait_send()
        w_c(q).wait_send()

    def finish_step(k):
        for side in range(2):
            h_direct(k, side).wait_send()
            h_forward(k, side).wait_send()

        @pl.loop(0, NQ)
        def _(q):
            for side in range(2):
                ring(rsb, rs_s, rs_r, q, k, side).wait_send()
                ring(yb, ag_s, ag_r, q, k, side).wait_send()

    def finish_part(k):
        for o in (1, 2, 3):
            part_x(k, o).wait_send()

    q_c_in().wait_recv()
    for i in range(2 * NY):
        packed = [wqp[o, i, 256:384] for o in range(NX)]
        for j in range(2):
            kvw[i * 256 + j * 128 : i * 256 + (j + 1) * 128] = jnp.concatenate(
                [p[:, j * 64 : (j + 1) * 64] for p in packed], axis=1
            )

    @pl.loop(0, NZ)
    def _(k):
        @pl.when(k > 0)
        def _():
            @pl.loop(0, NQ)
            def _(q):
                gather_step(q, k)

        project_step(k)

        @pl.when(k >= 2)
        def _():
            combine_step(k - 2)
            finish_part(k - 2)

        @pl.when(k > 0)
        def _():
            finish_step(k - 1)

        @pl.when((k > 1) & (k < NQ + 2))
        def _():
            finish_quarter(k - 2)

        @pl.when(k == 1)
        def _():
            for o in (1, 2, 3):
                q_x(o).wait_send()
                res_x(o).wait_send()
            for side in range(2):
                q_y(side).wait_send()
                q_forward(side).wait_send()
                h_direct(NZ - 1, side).wait_send()
                h_forward(NZ - 1, side).wait_send()
            q_c().wait_send()

    @pl.loop(NZ - 2, NZ)
    def _(k):
        combine_step(k)
        finish_part(k)


def per_device(
    hidden,
    residual,
    down_weight,
    norm_gain,
    query_codes,
    query_scales,
    pair_codes,
    pair_scales,
    input_groups,
    query_bias,
    pair_bias,
):
    depth = hidden.shape[1]
    wide_depth = (depth + 127) // 128 * 128
    dma = pltpu.SemaphoreType.DMA
    pairs = []
    for shape in (
        (8, 4), (NQ, 3), (NQ, 4), (NQ,), (3,), (4,), (1,),
        (3,), (NQ, 7, 2), (NQ, 7, 2), (NQ, 3), (8, 3),
    ):
        pairs += [dma(shape), dma(shape)]
    new_residual, queries, key_values = pl.pallas_call(
        kernel,
        out_shape=(
            pltpu.VMEM(residual.shape, BF16),
            pltpu.VMEM((4, 8, 32, 128), BF16),
            pltpu.VMEM((2, 4, 8, 32, 32), BF16),
        ),
        in_specs=[pl.BlockSpec(memory_space=pl.ANY)] * 5 + [pl.BlockSpec(memory_space=pltpu.VMEM)] * 6,
        out_specs=(
            pl.BlockSpec(memory_space=pltpu.VMEM),
            pl.BlockSpec(memory_space=pltpu.VMEM),
            pl.BlockSpec(memory_space=pltpu.VMEM),
        ),
        scratch_shapes=[
            pltpu.VMEM((NQ, NX, 4, depth, 128), BF16),
            pltpu.VMEM((NX, NZ, 4, 32, wide_depth), BF16),
            pltpu.VMEM((NQ, NZ, 4, 32, QW), BF16),
            pltpu.VMEM((NQ, NZ, 4, 32, QW), BF16),
            pltpu.VMEM((NX, 384, 128), BF16),
            pltpu.VMEM((NX, 256, 128), BF16),
            pltpu.VMEM((NX, 2, 32, 256), BF16),
            pltpu.VMEM((NX, 8, 384, 128), BF16),
            pltpu.VMEM((XW, 256), BF16),
            pltpu.VMEM((3, NZ, 128, 256), BF16),
            pltpu.VMEM((NZ, NX, 128, 256), BF16),
            pltpu.VMEM((4, 32, XW), BF16),
            pltpu.VMEM((NX * XW // 128, 128), F32),
            pltpu.VMEM((depth, 1024), BF16),
            dma((1,)), dma((NQ, 4)), dma((1,)), dma((1,)), dma((NQ,)), dma((NX, 2)),
        ] + pairs,
        compiler_params=pltpu.CompilerParams(
            collective_id=0, has_side_effects=True, vmem_limit_bytes=58 * 2**20
        ),
        cost_estimate=pl.CostEstimate(flops=12_000_000_000, bytes_accessed=14_000_000, transcendentals=0),
    )(
        hidden.T,
        residual,
        down_weight,
        query_codes,
        jnp.transpose(pair_codes, (0, 2, 1)),
        input_groups.reshape(-1, 128),
        norm_gain.reshape(-1, 128),
        query_scales,
        jnp.transpose(pair_scales, (0, 2, 1)),
        query_bias.reshape(1, 128),
        pair_bias,
    )
    return new_residual, queries.reshape(1024, 128), key_values.reshape(2, 1024, 32)


def solution(mesh):
    in_specs = (
        P("dp", "tensor"),
        P(("dp", "tensor"), None),
        P("tensor", None),
        P(),
        P(None, "tensor"),
        P(None, "tensor"),
        P(None, None, "tensor"),
        P(None, None, "tensor"),
        P(),
        P("tensor"),
        P(None, "tensor"),
    )
    out_specs = (P(("dp", "tensor"), None), P("dp", "tensor"), P(None, "dp", "tensor"))
    return jax.shard_map(
        per_device, mesh=mesh, in_specs=in_specs, out_specs=out_specs, check_vma=False
    )
```
